32 devices in a mesh: row: 8 (over z, x), col: 4 (over y, core).
Axes of the slice: x: 2, y: 2, z: 4, core: 2. Of those that a mesh axis runs over, the one named last changes fastest.
Arguments:
- slab: float32 [2048, 131072], P('col', 'row'), may hold values from -6 to 6
- stored: float32 [32, 131072], P(('row', 'col')), may hold values from -6 to 6
- owner: int32 [4], replicated, may hold values from 0 to 31
Outputs:
- result: float32 [2048, 131072], P('col', 'row')
The draws below stay inside these ranges and needn't reach their ends.
All inputs are finite; a program needn't handle non-finite values.
Results may differ from the reference program's by a relative error of at most 0.0001.
Values sent between devices are 32-bit elements; how exact they have to be, the bound alone decides.
No kernel may reach another device: no remote copies, remote signals or barrier semaphores. Data moves between devices by JAX's collectives and lax.ppermute only.
A program may use at most 256 MiB of HBM per device.

```python
import jax
import jax.numpy as jnp
from jax import lax

ORDER = 131072
EIGVECS = 2048
BAND = 64
GROUPS = 4
N_ROW = 8
N_COL = 4
DEVICES = 32


def plant(drawn, key, least, high):
    index_at = [jax.random.randint(jax.random.fold_in(key, axis), (), 0, length) for axis, length in enumerate(drawn.shape)]
    widest = drawn.shape.index(max(drawn.shape))
    next_to = index_at[:widest] + [(index_at[widest] + 1) % drawn.shape[widest]] + index_at[widest + 1:]
    return drawn.at[tuple(index_at)].set(least).at[tuple(next_to)].set(high)


def level_of(key, dims, shards, least, high):
    def one(axis_at, blocks):
        draws = jax.random.uniform(jax.random.fold_in(jax.random.fold_in(key, 6), axis_at), (blocks,), jnp.float32, least / len(shards), high / len(shards))
        return jnp.repeat(jnp.exp(draws), dims[axis_at] // blocks).reshape((-1,) + (1,) * (len(dims) - axis_at - 1))

    gain = one(*shards[0])
    for cut in shards[1:]:
        gain = gain * one(*cut)
    return gain


def bell_draw(rng, dims, scale, reach, shards=(), held_as=jnp.bfloat16):
    values = scale * jax.random.normal(rng, dims, jnp.float32)
    if shards:
        values = values * level_of(rng, dims, shards, -0.22, 0.18)
    return jnp.clip(values, -reach, reach).astype(held_as)


def setup_inputs(seed: int = 0) -> dict:
    key_of = jax.random.split(jax.random.key(seed), 4)
    slab = bell_draw(key_of[0], (EIGVECS, ORDER), 1.0, 6.0, ((0, 4), (1, 8)), jnp.float32)
    stored = bell_draw(key_of[1], (DEVICES, ORDER), 1.0, 6.0, ((0, 32),), jnp.float32)
    owner = plant(jax.random.randint(key_of[2], (GROUPS,), 0, DEVICES), jax.random.fold_in(key_of[2], 1), 0, DEVICES - 1).astype(jnp.int32)
    return {"slab": slab, "stored": stored, "owner": owner}


def offset_of(group):
    return 1 + (37 * group + 11) % 63


def reference(slab, stored, owner):
    parts = N_ROW
    tiles = ORDER // (parts * BAND)
    count = ORDER // BAND
    span = (count - 1) * BAND
    vectors = []
    for group in range(GROUPS):
        vectors.append(lax.dynamic_index_in_dim(stored, owner[group], 0, keepdims=False))

    def apply_block(block):
        rows = block.shape[0]
        natural = block.reshape(rows, parts, tiles, BAND).transpose(0, 2, 1, 3).reshape(rows, ORDER)
        for group in range(GROUPS):
            start = offset_of(group)
            vwin = vectors[group][start:start + span].reshape(count - 1, BAND)
            tau = 2.0 / (jnp.sum(vwin * vwin, axis=-1) + 1e-6)
            middle = natural[:, start:start + span].reshape(rows, count - 1, BAND)
            inner = jnp.sum(middle * vwin[None], axis=-1)
            middle = middle - (inner * tau[None])[:, :, None] * vwin[None]
            natural = jnp.concatenate([natural[:, :start], middle.reshape(rows, span), natural[:, start + span:]], axis=1)
        return natural.reshape(rows, tiles, parts, BAND).transpose(0, 2, 1, 3).reshape(rows, ORDER)

    blocks = slab.reshape(N_COL, EIGVECS // N_COL, ORDER)
    return lax.map(apply_block, blocks).reshape(EIGVECS, ORDER)
```

```python
import functools

import jax
import jax.numpy as jnp
import numpy as np
from jax import lax
from jax.experimental import pallas as pl
from jax.experimental.pallas import tpu as pltpu
from jax.sharding import PartitionSpec as P

BAND = 64
GROUPS = 4
LANES = 128
BLOCK = 8 * BAND
CHUNKS = 2
MIB = 1 << 20
HIGH = lax.Precision.HIGHEST
PAIRS = [(g, h) for g in range(GROUPS) for h in range(g)]
NORM = 4 * len(PAIRS)


def offset_of(group):
    return 1 + (37 * group + 11) % 63


def swap(block, axis, bit):
    size = lax.axis_size(axis)
    return lax.ppermute(block, axis, [(i, i ^ bit) for i in range(size)])


def swap_first(block):
    return swap(block, "row", 1)


def swap_second(block):
    size = lax.axis_size("row")
    route = [(i, (i + 1) % size if i % 2 else (i - 1) % size) for i in range(size)]
    return lax.ppermute(block, "row", route)


def params(mib):
    return pltpu.CompilerParams(vmem_limit_bytes=mib * MIB)


def vmem():
    return pl.BlockSpec(memory_space=pltpu.VMEM)


def smem():
    return pl.BlockSpec(memory_space=pltpu.SMEM)


def deal_kernel(parts, row_ref, out_ref):
    pairs = out_ref.shape[1]
    lane = lax.broadcasted_iota(jnp.int32, (pairs, LANES), 1)
    for q in range(parts // 2):
        one = row_ref[pl.ds(q, pairs, stride=parts), :]
        two = row_ref[pl.ds(q + parts // 2, pairs, stride=parts), :]
        out_ref[2 * q] = jnp.where(lane < BAND, one, pltpu.roll(two, BAND, 1))
        out_ref[2 * q + 1] = jnp.where(lane < BAND, pltpu.roll(one, BAND, 1), two)


def deal(row, parts):
    pairs = row.shape[0] // parts
    return pl.pallas_call(
        functools.partial(deal_kernel, parts),
        out_shape=jax.ShapeDtypeStruct((parts, pairs, LANES), jnp.float32),
        in_specs=[vmem()],
        out_specs=vmem(),
        compiler_params=params(16),
        name="deal",
    )(row)


def pick_kernel(n_col, owner_ref, here_ref, got_ref, keep_ref, give_ref):
    half = keep_ref.shape[1]
    col = here_ref[0]
    core = col % 2
    for g in range(GROUPS):
        owner = owner_ref[g]
        mine = jnp.where(owner % n_col == col, 1.0, 0.0).astype(jnp.float32)
        at = owner // n_col
        keep_ref[g] = jnp.where(mine > 0, got_ref[at, pl.ds(core * half, half), :], 0.0)
        give_ref[g] = jnp.where(mine > 0, got_ref[at, pl.ds((1 - core) * half, half), :], 0.0)


def pick(owner, here, got, n_col):
    half = got.shape[1] // 2
    shape = jax.ShapeDtypeStruct((GROUPS, half, LANES), jnp.float32)
    return pl.pallas_call(
        functools.partial(pick_kernel, n_col),
        out_shape=(shape, shape),
        in_specs=[smem(), smem(), vmem()],
        out_specs=(vmem(), vmem()),
        compiler_params=params(16),
        name="pick",
    )(owner, here, got)


def fetch_vectors(stored, owner):
    parts, n_col = lax.axis_size("row"), lax.axis_size("col")
    col = lax.axis_index("col")
    rows = deal(stored.reshape(-1, LANES), parts)
    got = lax.all_to_all(rows, "row", 0, 0)
    keep, give = pick(owner, col.reshape(1), got, n_col)
    keep = keep + swap(give, "col", 1)
    bit = 2
    while bit < n_col:
        keep = keep + swap(keep, "col", bit)
        bit *= 2
    return keep, swap(keep, "col", 1)


def first_lanes(parity, group, lane):
    return jnp.where(lane >= offset_of(group), 1, 0) != parity


def table_kernel(here_ref, keep_ref, other_ref, v_ref, table_ref, norms_ref, tiles_ref):
    half = keep_ref.shape[1]
    core, parity = here_ref[0] % 2, here_ref[1] % 2
    for g in range(GROUPS):
        v_ref[g, pl.ds(core * half, half), :] = keep_ref[g]
        v_ref[g, pl.ds((1 - core) * half, half), :] = other_ref[g]
    for g in range(GROUPS):
        pairs = v_ref[g]
        tiles_ref[g, pl.ds(0, 2 * half, stride=2), :] = pairs
        tiles_ref[g, pl.ds(1, 2 * half, stride=2), :] = pltpu.roll(pairs, BAND, 1)
    lane = lax.broadcasted_iota(jnp.int32, (LANES, LANES), 0)
    col = lax.broadcasted_iota(jnp.int32, (LANES, LANES), 1)
    valid = lane < BAND
    first = [first_lanes(parity, g, lane) for g in range(GROUPS)]
    table = jnp.zeros(table_ref.shape, jnp.float32)
    for at, (g, h) in enumerate(PAIRS):
        base = 4 * at
        spot = base + jnp.where(first[g], 0, 2) + jnp.where(first[h], 0, 1)
        hit = valid & (col == spot)
        table += jnp.dot(
            tiles_ref[g] * tiles_ref[h],
            jnp.where(hit, 1.0, 0.0).astype(jnp.float32),
            precision=HIGH,
            preferred_element_type=jnp.float32,
        )
    for g in range(GROUPS):
        spot = jnp.where(first[g], NORM + g, NORM + GROUPS + g)
        hit = valid & (col == spot)
        table += jnp.dot(
            tiles_ref[g] * tiles_ref[g],
            jnp.where(hit, 1.0, 0.0).astype(jnp.float32),
            precision=HIGH,
            preferred_element_type=jnp.float32,
        )
    table_ref[...] = table
    turned = jnp.transpose(table)
    norms_ref[0] = turned[NORM : NORM + 8]
    norms_ref[1] = pltpu.roll(turned[NORM : NORM + 8], GROUPS, 0)


def make_table(here, keep, other):
    _, half, _ = keep.shape
    tiles = 4 * half
    return pl.pallas_call(
        table_kernel,
        out_shape=(
            jax.ShapeDtypeStruct((GROUPS, 2 * half, LANES), jnp.float32),
            jax.ShapeDtypeStruct((tiles, LANES), jnp.float32),
            jax.ShapeDtypeStruct((2, 8, tiles), jnp.float32),
        ),
        in_specs=[smem(), vmem(), vmem()],
        out_specs=(vmem(), vmem(), vmem()),
        scratch_shapes=[pltpu.VMEM((GROUPS, tiles, LANES), jnp.float32)],
        compiler_params=params(16),
        name="table",
    )(here, keep, other)


def pieces(parity, v_ref):
    lane = lax.broadcasted_iota(jnp.int32, (8, BLOCK), 1)
    tile = lax.broadcasted_iota(jnp.int32, (8, BLOCK), 0)
    own = lane // BAND == tile
    first, second = [], []
    for g in range(GROUPS):
        wide = jnp.concatenate(
            [jnp.broadcast_to(v_ref[g, j : j + 1, :], (8, LANES)) for j in range(BLOCK // LANES)], axis=1
        )
        hit = first_lanes(parity, g, lane % BAND)
        first.append(jnp.where(own & hit, wide, 0.0))
        second.append(jnp.where(own & jnp.logical_not(hit), wide, 0.0))
    return jnp.concatenate(first + second, axis=0)


def split(x):
    high = x.astype(jnp.bfloat16)
    return high, (x - high.astype(jnp.float32)).astype(jnp.bfloat16)


def products_kernel(blocks, here_ref, v_ref, x_ref, norms_ref, one_ref, two_ref, rest_ref):
    step = pl.program_id(0)

    @pl.when(step < blocks)
    def _():
        w_high, w_low = split(pieces(here_ref[1] % 2, v_ref))
        x_high, x_low = split(x_ref[...])
        across = (((1,), (1,)), ((), ()))
        both = lax.dot_general(
            jnp.concatenate([w_high, w_low], axis=0), x_high, across, preferred_element_type=jnp.float32
        )
        low = lax.dot_general(w_high, x_low, across, preferred_element_type=jnp.float32)
        sums = both[:64] + both[64:] + low
        one_ref[...] = sums[0:8]
        two_ref[...] = sums[32:40]
        for g in range(1, GROUPS):
            rest_ref[g - 1] = sums[8 * g : 8 * g + 8]
            rest_ref[g + 2] = sums[32 + 8 * g : 40 + 8 * g]

    @pl.when(step >= blocks)
    def _():
        one_ref[...] = norms_ref[0]
        two_ref[...] = norms_ref[1]


def products(here, v, slab, norms, chunk, width):
    blocks = slab.shape[1] // BLOCK
    extra = norms.shape[0] if chunk == 0 else 0
    tiles = 8 * blocks
    last = blocks - 1
    message = jax.ShapeDtypeStruct((tiles + 8 * extra, width), jnp.float32)
    return pl.pallas_call(
        functools.partial(products_kernel, blocks),
        grid=(blocks + extra,),
        out_shape=(message, message, jax.ShapeDtypeStruct((2 * GROUPS - 2, tiles, width), jnp.float32)),
        in_specs=[
            smem(),
            pl.BlockSpec((GROUPS, None, BLOCK // LANES, LANES), lambda b: (0, jnp.minimum(b, last), 0, 0)),
            pl.BlockSpec((width, BLOCK), lambda b: (chunk, jnp.minimum(b, last))),
            pl.BlockSpec((None, 2, 8, width), lambda b: (jnp.maximum(b - blocks, 0), 0, 0, 0)),
        ],
        out_specs=(
            pl.BlockSpec((8, width), lambda b: (b, 0)),
            pl.BlockSpec((8, width), lambda b: (b, 0)),
            pl.BlockSpec((2 * GROUPS - 2, 8, width), lambda b: (0, jnp.minimum(b, last), 0)),
        ),
        compiler_params=params(32),
        cost_estimate=pl.CostEstimate(
            flops=2 * 192 * width * slab.shape[1], bytes_accessed=4 * width * slab.shape[1], transcendentals=0
        ),
        name="products",
    )(here, v, slab, norms)


def align(x, here_ref):
    back = jnp.concatenate([x[1:], x[:1]], axis=0)
    on = jnp.concatenate([x[-1:], x[:-1]], axis=0)
    return jnp.where(here_ref[1] == 0, on, jnp.where(here_ref[1] == here_ref[2] - 1, back, x))


def scales_of(here_ref, table_ref, got_one_ref, got_two_ref):
    tiles = table_ref.shape[0]
    got = []
    for ref in (got_one_ref, got_two_ref):
        rows = [ref[at : at + 8, :] for at in range(tiles, ref.shape[0], 8)]
        rows = jnp.concatenate(rows, axis=1)[:, :tiles]
        got.append(jnp.transpose(jnp.concatenate([rows] + [jnp.zeros_like(rows)] * (LANES // 8 - 1), axis=0)))
    row = lax.broadcasted_iota(jnp.int32, (tiles, LANES), 0)
    gone = ((here_ref[1] == 0) & (row == 0)) | ((here_ref[1] == here_ref[2] - 1) & (row == tiles - 1))
    col = lax.broadcasted_iota(jnp.int32, (tiles, LANES), 1)
    other = jnp.where(col < GROUPS, got[0], pltpu.roll(align(got[1], here_ref), GROUPS, 1))
    own = pltpu.roll(table_ref[...], LANES - NORM, 1)
    tau = 2.0 / (own + other + 1e-6)
    return jnp.where(gone & (col >= GROUPS), 0.0, tau)


def solve_kernel(group, lead, *refs):
    refs = list(refs)
    here_ref, table_ref = refs.pop(0), refs.pop(0)
    tau_ref = None if lead else refs.pop(0)
    own_one_ref, own_two_ref, got_one_ref, got_two_ref = [refs.pop(0) for _ in range(4)]
    last = group == GROUPS - 1
    rest_ref = None if last else refs.pop(0)
    before = [refs.pop(0) for _ in range(2 * group)]
    tiles = table_ref.shape[0]
    if lead:
        tau = scales_of(here_ref, table_ref, got_one_ref, got_two_ref)
    else:
        tau = tau_ref[...]
    coef_one_ref, coef_two_ref = refs.pop(0), refs.pop(0)
    one = tau[:, group : group + 1] * (own_one_ref[:tiles] + got_one_ref[:tiles])
    two = tau[:, GROUPS + group : GROUPS + group + 1] * (
        own_two_ref[:tiles] + align(got_two_ref[:tiles], here_ref)
    )
    coef_one_ref[...] = one
    coef_two_ref[...] = two
    if not last:
        next_one_ref, next_two_ref = refs.pop(0), refs.pop(0)
        table = table_ref[...]
        later = group + 1
        next_one = rest_ref[later - 1]
        next_two = rest_ref[later + 2]
        for h in range(later):
            at = 4 * PAIRS.index((later, h))
            c_one, c_two = (one, two) if h == group else (before[2 * h][...], before[2 * h + 1][...])
            next_one = next_one - table[:, at : at + 1] * c_one - table[:, at + 1 : at + 2] * c_two
            next_two = next_two - table[:, at + 2 : at + 3] * c_one - table[:, at + 3 : at + 4] * c_two
        next_one_ref[...] = next_one
        next_two_ref[...] = next_two
    if lead:
        refs.pop(0)[...] = tau


def solve(here, table, tau, own, got, rest, before, group):
    tiles, width = table.shape[0], own[0].shape[1]
    lead = tau is None
    last = group == GROUPS - 1
    inputs = [here, table] + ([] if lead else [tau]) + list(own) + list(got)
    if not last:
        inputs.append(rest)
    inputs += [c for pair in before for c in pair]
    shape = jax.ShapeDtypeStruct((tiles, width), jnp.float32)
    shapes = [shape, shape] + ([] if last else [shape, shape])
    if lead:
        shapes.append(jax.ShapeDtypeStruct((tiles, LANES), jnp.float32))
    return pl.pallas_call(
        functools.partial(solve_kernel, group, lead),
        out_shape=tuple(shapes),
        in_specs=[smem()] + [vmem()] * (len(inputs) - 1),
        out_specs=tuple(vmem() for _ in shapes),
        compiler_params=params(24),
        cost_estimate=pl.CostEstimate(
            flops=8 * tiles * width, bytes_accessed=4 * tiles * width * (len(inputs) + 2), transcendentals=0
        ),
        name="solve",
    )(*inputs)


def update_kernel(here_ref, v_ref, x_ref, *refs):
    out_ref = refs[-1]
    coefs = jnp.concatenate([ref[...] for ref in refs[: 2 * GROUPS]], axis=0)
    c_high, c_low = split(coefs)
    w_high, w_low = split(pieces(here_ref[1] % 2, v_ref))
    change = lax.dot_general(
        jnp.concatenate([c_high, c_high, c_low], axis=0),
        jnp.concatenate([w_high, w_low, w_high], axis=0),
        (((0,), (0,)), ((), ())),
        preferred_element_type=jnp.float32,
    )
    out_ref[...] = x_ref[...] - change


def update(here, v, slab, coefs, result, chunk, width):
    blocks = slab.shape[1] // BLOCK
    ordered = [c[0] for c in coefs] + [c[1] for c in coefs]
    inputs = [here, v, slab] + ordered
    specs = [
        smem(),
        pl.BlockSpec((GROUPS, None, BLOCK // LANES, LANES), lambda b: (0, b, 0, 0)),
        pl.BlockSpec((width, BLOCK), lambda b: (chunk, b)),
    ] + [pl.BlockSpec((8, width), lambda b: (b, 0))] * (2 * GROUPS)
    alias = {}
    if result is not None:
        alias = {len(inputs): 0}
        inputs.append(result)
        specs.append(pl.BlockSpec(memory_space=pl.ANY))
    return pl.pallas_call(
        update_kernel,
        grid=(blocks,),
        out_shape=jax.ShapeDtypeStruct(slab.shape, jnp.float32),
        in_specs=specs,
        out_specs=pl.BlockSpec((width, BLOCK), lambda b: (chunk, b)),
        input_output_aliases=alias,
        compiler_params=params(32),
        cost_estimate=pl.CostEstimate(
            flops=2 * 192 * width * slab.shape[1], bytes_accessed=8 * width * slab.shape[1], transcendentals=0
        ),
        name="update",
    )(*inputs)


def shards(slab, stored, owner):
    parts = lax.axis_size("row")
    columns, rows = slab.shape
    tiles = rows // BAND
    width = columns // CHUNKS
    here = jnp.stack([lax.axis_index("col"), lax.axis_index("row"), jnp.int32(parts)]).astype(jnp.int32)
    keep, other = fetch_vectors(stored, owner)
    v, table, norms = make_table(here, keep, other)
    v = v.reshape(GROUPS, rows // BLOCK, BLOCK // LANES, LANES)
    if tiles < width:
        norms = jnp.pad(norms, ((0, 0), (0, 0), (0, width - tiles)))
    norms = norms.reshape(2, 8, -1, width).transpose(2, 0, 1, 3)
    own, rest, coefs = [], [], [[] for _ in range(CHUNKS)]
    for chunk in range(CHUNKS):
        one, two, more = products(here, v, slab, norms, chunk, width)
        own.append((one, two))
        rest.append(more)
    tau = None
    for group in range(GROUPS):
        for chunk in range(CHUNKS):
            got = (swap_first(own[chunk][0]), swap_second(own[chunk][1]))
            outs = solve(here, table, tau, own[chunk], got, rest[chunk], coefs[chunk], group)
            coefs[chunk].append(outs[:2])
            if group < GROUPS - 1:
                own[chunk] = outs[2:4]
            if tau is None:
                tau = outs[-1]
    result = None
    for chunk in range(CHUNKS):
        result = update(here, v, slab, coefs[chunk], result, chunk, width)
    return result


def solution(mesh):
    placed = (P("col", "row"), P(("row", "col"), None), P())
    return jax.shard_map(
        shards, mesh=mesh, in_specs=placed, out_specs=P("col", "row"), check_vma=False
    )
```

```python
import functools

import jax
import jax.numpy as jnp
import numpy as np
from jax import lax
from jax.experimental import pallas as pl
from jax.experimental.pallas import tpu as pltpu
from jax.sharding import PartitionSpec as P

BAND = 64
GROUPS = 4
LANES = 128
BLOCK = 8 * BAND
CHUNKS = 2
LOADS = 8
SPAN = 8 * BLOCK
MIB = 1 << 20
HIGH = lax.Precision.HIGHEST
PAIRS = [(g, h) for g in range(GROUPS) for h in range(g)]
NORM = 4 * len(PAIRS)


def offset_of(group):
    return 1 + (37 * group + 11) % 63


def swap(block, axis, bit):
    size = lax.axis_size(axis)
    return lax.ppermute(block, axis, [(i, i ^ bit) for i in range(size)])


def swap_first(block):
    return swap(block, "row", 1)


def swap_second(block):
    size = lax.axis_size("row")
    route = [(i, (i + 1) % size if i % 2 else (i - 1) % size) for i in range(size)]
    return lax.ppermute(block, "row", route)


def params(mib):
    return pltpu.CompilerParams(vmem_limit_bytes=mib * MIB)


def vmem():
    return pl.BlockSpec(memory_space=pltpu.VMEM)


def smem():
    return pl.BlockSpec(memory_space=pltpu.SMEM)


def deal_kernel(parts, here_ref, row_ref, *out_refs):
    pairs = out_refs[0].shape[0]
    lane = lax.broadcasted_iota(jnp.int32, (pairs, LANES), 1)
    for s, out_ref in enumerate(out_refs):
        to = here_ref[1] ^ s
        one = row_ref[pl.ds(to // 2, pairs, stride=parts), :]
        two = row_ref[pl.ds(to // 2 + parts // 2, pairs, stride=parts), :]
        even = jnp.where(lane < BAND, one, pltpu.roll(two, BAND, 1))
        odd = jnp.where(lane < BAND, pltpu.roll(one, BAND, 1), two)
        out_ref[...] = jnp.where(to % 2 == 0, even, odd)


def deal(here, row, parts):
    pairs = row.shape[0] // parts
    shape = jax.ShapeDtypeStruct((pairs, LANES), jnp.float32)
    return pl.pallas_call(
        functools.partial(deal_kernel, parts),
        out_shape=(shape,) * parts,
        in_specs=[smem(), vmem()],
        out_specs=(vmem(),) * parts,
        compiler_params=params(8),
        name="deal",
    )(here, row)


def pick_kernel(n_col, owner_ref, here_ref, *refs):
    keep_ref, give_ref = refs[-2:]
    half = keep_ref.shape[1]
    col, row = here_ref[0], here_ref[1]
    core = col % 2
    keep_ref[...] = jnp.zeros(keep_ref.shape, jnp.float32)
    give_ref[...] = jnp.zeros(give_ref.shape, jnp.float32)
    for g in range(GROUPS):
        owner = owner_ref[g]
        for s, got_ref in enumerate(refs[:-2]):

            @pl.when((owner % n_col == col) & (owner // n_col == row ^ s))
            def _():
                keep_ref[g] = got_ref[pl.ds(core * half, half), :]
                give_ref[g] = got_ref[pl.ds((1 - core) * half, half), :]


def pick(owner, here, got, n_col):
    half = got[0].shape[0] // 2
    shape = jax.ShapeDtypeStruct((GROUPS, half, LANES), jnp.float32)
    return pl.pallas_call(
        functools.partial(pick_kernel, n_col),
        out_shape=(shape, shape),
        in_specs=[smem(), smem()] + [vmem()] * len(got),
        out_specs=(vmem(), vmem()),
        compiler_params=params(8),
        name="pick",
    )(owner, here, *got)


def fetch_vectors(here, stored, owner):
    parts, n_col = lax.axis_size("row"), lax.axis_size("col")
    rows = deal(here, stored.reshape(-1, LANES), parts)
    got = [rows[0]] + [swap(rows[s], "row", s) for s in range(1, parts)]
    keep, give = pick(owner, here, got, n_col)
    keep = keep + swap(give, "col", 1)
    bit = 2
    while bit < n_col:
        keep = keep + swap(keep, "col", bit)
        bit *= 2
    return keep, swap(keep, "col", 1)


def first_lanes(parity, group, lane):
    return jnp.where(lane >= offset_of(group), 1, 0) != parity


def table_kernel(here_ref, keep_ref, other_ref, v_ref, table_ref, norms_ref, tiles_ref):
    half = keep_ref.shape[1]
    core, parity = here_ref[0] % 2, here_ref[1] % 2
    for g in range(GROUPS):
        v_ref[g, pl.ds(core * half, half), :] = keep_ref[g]
        v_ref[g, pl.ds((1 - core) * half, half), :] = other_ref[g]
    for g in range(GROUPS):
        pairs = v_ref[g]
        tiles_ref[g, pl.ds(0, 2 * half, stride=2), :] = pairs
        tiles_ref[g, pl.ds(1, 2 * half, stride=2), :] = pltpu.roll(pairs, BAND, 1)
    lane = lax.broadcasted_iota(jnp.int32, (LANES, LANES), 0)
    col = lax.broadcasted_iota(jnp.int32, (LANES, LANES), 1)
    valid = lane < BAND
    first = [first_lanes(parity, g, lane) for g in range(GROUPS)]
    table = jnp.zeros(table_ref.shape, jnp.float32)
    for at, (g, h) in enumerate(PAIRS):
        base = 4 * at
        spot = base + jnp.where(first[g], 0, 2) + jnp.where(first[h], 0, 1)
        hit = valid & (col == spot)
        table += jnp.dot(
            tiles_ref[g] * tiles_ref[h],
            jnp.where(hit, 1.0, 0.0).astype(jnp.float32),
            precision=HIGH,
            preferred_element_type=jnp.float32,
        )
    for g in range(GROUPS):
        spot = jnp.where(first[g], NORM + g, NORM + GROUPS + g)
        hit = valid & (col == spot)
        table += jnp.dot(
            tiles_ref[g] * tiles_ref[g],
            jnp.where(hit, 1.0, 0.0).astype(jnp.float32),
            precision=HIGH,
            preferred_element_type=jnp.float32,
        )
    table_ref[...] = table
    turned = jnp.transpose(table)
    norms_ref[0] = turned[NORM : NORM + 8]
    norms_ref[1] = pltpu.roll(turned[NORM : NORM + 8], GROUPS, 0)


def make_table(here, keep, other):
    _, half, _ = keep.shape
    tiles = 4 * half
    return pl.pallas_call(
        table_kernel,
        out_shape=(
            jax.ShapeDtypeStruct((GROUPS, 2 * half, LANES), jnp.float32),
            jax.ShapeDtypeStruct((tiles, LANES), jnp.float32),
            jax.ShapeDtypeStruct((2, 8, tiles), jnp.float32),
        ),
        in_specs=[smem(), vmem(), vmem()],
        out_specs=(vmem(), vmem(), vmem()),
        scratch_shapes=[pltpu.VMEM((GROUPS, tiles, LANES), jnp.float32)],
        compiler_params=params(8),
        name="table",
    )(here, keep, other)


def load_kernel(chunk, x_ref, out_ref, sems):
    rows = out_ref.shape[0] // LOADS
    start = chunk * out_ref.shape[0]
    copies = [
        pltpu.make_async_copy(
            x_ref.at[pl.ds(start + i * rows, rows)], out_ref.at[pl.ds(i * rows, rows)], sems.at[i]
        )
        for i in range(LOADS)
    ]
    for copy in copies:
        copy.start()
    for copy in copies:
        copy.wait()


def load(slab, chunk, width):
    return pl.pallas_call(
        functools.partial(load_kernel, chunk),
        out_shape=jax.ShapeDtypeStruct((width, slab.shape[1]), slab.dtype),
        in_specs=[pl.BlockSpec(memory_space=pl.ANY)],
        out_specs=vmem(),
        scratch_shapes=[pltpu.SemaphoreType.DMA((LOADS,))],
        compiler_params=params(28),
        cost_estimate=pl.CostEstimate(flops=0, bytes_accessed=8 * width * slab.shape[1], transcendentals=0),
        name="load",
    )(slab)


def piece_masks(parity):
    lane = lax.broadcasted_iota(jnp.int32, (8, BLOCK), 1)
    tile = lax.broadcasted_iota(jnp.int32, (8, BLOCK), 0)
    own = lane // BAND == tile
    hits = [first_lanes(parity, g, lane % BAND) for g in range(GROUPS)]
    first = [jnp.where(own & hit, 1.0, 0.0).astype(jnp.float32) for hit in hits]
    second = [jnp.where(own & jnp.logical_not(hit), 1.0, 0.0).astype(jnp.float32) for hit in hits]
    return first, second


def pieces(masks, v_ref, block):
    rows = BLOCK // LANES
    wide = [
        jnp.concatenate(
            [jnp.broadcast_to(v_ref[g, pl.ds(rows * block + j, 1), :], (8, LANES)) for j in range(rows)], axis=1
        )
        for g in range(GROUPS)
    ]
    return jnp.concatenate([m * w for kind in masks for m, w in zip(kind, wide)], axis=0)


def split(x):
    high = x.astype(jnp.bfloat16)
    return high, (x - high.astype(jnp.float32)).astype(jnp.bfloat16)


def products_kernel(here_ref, v_ref, x_ref, norms_ref, one_ref, two_ref, rest_ref):
    width = one_ref.shape[1]
    tiles = rest_ref.shape[1]
    masks = piece_masks(here_ref[1] % 2)

    @pl.loop(0, tiles // 8, unroll=4)
    def _(block):
        w_high, w_low = split(pieces(masks, v_ref, block))
        x_high, x_low = split(x_ref[:, pl.ds(block * BLOCK, BLOCK)])
        across = (((1,), (1,)), ((), ()))
        both = lax.dot_general(
            jnp.concatenate([w_high, w_low], axis=0), x_high, across, preferred_element_type=jnp.float32
        )
        low = lax.dot_general(w_high, x_low, across, preferred_element_type=jnp.float32)
        sums = both[:64] + both[64:] + low
        spot = pl.ds(block * 8, 8)
        one_ref[spot, :] = sums[0:8]
        two_ref[spot, :] = sums[32:40]
        for g in range(1, GROUPS):
            rest_ref[g - 1, spot, :] = sums[8 * g : 8 * g + 8]
            rest_ref[g + 2, spot, :] = sums[32 + 8 * g : 40 + 8 * g]

    for at in range((one_ref.shape[0] - tiles) // 8):
        one_ref[tiles + 8 * at : tiles + 8 * at + 8] = norms_ref[at, 0]
        two_ref[tiles + 8 * at : tiles + 8 * at + 8] = norms_ref[at, 1]


def products(here, v, slab, norms, chunk):
    width, tiles = slab.shape[0], slab.shape[1] // BAND
    extra = norms.shape[0] if chunk == 0 else 0
    message = jax.ShapeDtypeStruct((tiles + 8 * extra, width), jnp.float32)
    return pl.pallas_call(
        products_kernel,
        out_shape=(message, message, jax.ShapeDtypeStruct((2 * GROUPS - 2, tiles, width), jnp.float32)),
        in_specs=[smem(), vmem(), vmem(), vmem()],
        out_specs=(vmem(), vmem(), vmem()),
        compiler_params=params(8),
        cost_estimate=pl.CostEstimate(
            flops=2 * 192 * width * slab.shape[1], bytes_accessed=4 * width * slab.shape[1], transcendentals=0
        ),
        name="products",
    )(here, v, slab, norms)


def align(x, here_ref):
    back = jnp.concatenate([x[1:], x[:1]], axis=0)
    on = jnp.concatenate([x[-1:], x[:-1]], axis=0)
    return jnp.where(here_ref[1] == 0, on, jnp.where(here_ref[1] == here_ref[2] - 1, back, x))


def scales_of(here_ref, table_ref, got_one_ref, got_two_ref):
    tiles = table_ref.shape[0]
    got = []
    for ref in (got_one_ref, got_two_ref):
        rows = [ref[at : at + 8, :] for at in range(tiles, ref.shape[0], 8)]
        rows = jnp.concatenate(rows, axis=1)[:, :tiles]
        got.append(jnp.transpose(jnp.concatenate([rows] + [jnp.zeros_like(rows)] * (LANES // 8 - 1), axis=0)))
    row = lax.broadcasted_iota(jnp.int32, (tiles, LANES), 0)
    gone = ((here_ref[1] == 0) & (row == 0)) | ((here_ref[1] == here_ref[2] - 1) & (row == tiles - 1))
    col = lax.broadcasted_iota(jnp.int32, (tiles, LANES), 1)
    other = jnp.where(col < GROUPS, got[0], pltpu.roll(align(got[1], here_ref), GROUPS, 1))
    own = pltpu.roll(table_ref[...], LANES - NORM, 1)
    tau = 2.0 / (own + other + 1e-6)
    return jnp.where(gone & (col >= GROUPS), 0.0, tau)


def solve_kernel(group, lead, *refs):
    refs = list(refs)
    here_ref, table_ref = refs.pop(0), refs.pop(0)
    tau_ref = None if lead else refs.pop(0)
    own_one_ref, own_two_ref, got_one_ref, got_two_ref = [refs.pop(0) for _ in range(4)]
    last = group == GROUPS - 1
    rest_ref = None if last else refs.pop(0)
    before = [refs.pop(0) for _ in range(2 * group)]
    tiles = table_ref.shape[0]
    if lead:
        tau = scales_of(here_ref, table_ref, got_one_ref, got_two_ref)
    else:
        tau = tau_ref[...]
    coef_one_ref, coef_two_ref = refs.pop(0), refs.pop(0)
    one = tau[:, group : group + 1] * (own_one_ref[:tiles] + got_one_ref[:tiles])
    two = tau[:, GROUPS + group : GROUPS + group + 1] * (
        own_two_ref[:tiles] + align(got_two_ref[:tiles], here_ref)
    )
    coef_one_ref[...] = one
    coef_two_ref[...] = two
    if not last:
        next_one_ref, next_two_ref = refs.pop(0), refs.pop(0)
        table = table_ref[...]
        later = group + 1
        next_one = rest_ref[later - 1]
        next_two = rest_ref[later + 2]
        for h in range(later):
            at = 4 * PAIRS.index((later, h))
            c_one, c_two = (one, two) if h == group else (before[2 * h][...], before[2 * h + 1][...])
            next_one = next_one - table[:, at : at + 1] * c_one - table[:, at + 1 : at + 2] * c_two
            next_two = next_two - table[:, at + 2 : at + 3] * c_one - table[:, at + 3 : at + 4] * c_two
        next_one_ref[...] = next_one
        next_two_ref[...] = next_two
    if lead:
        refs.pop(0)[...] = tau


def solve(here, table, tau, own, got, rest, before, group):
    tiles, width = table.shape[0], own[0].shape[1]
    lead = tau is None
    last = group == GROUPS - 1
    inputs = [here, table] + ([] if lead else [tau]) + list(own) + list(got)
    if not last:
        inputs.append(rest)
    inputs += [c for pair in before for c in pair]
    shape = jax.ShapeDtypeStruct((tiles, width), jnp.float32)
    shapes = [shape, shape] + ([] if last else [shape, shape])
    if lead:
        shapes.append(jax.ShapeDtypeStruct((tiles, LANES), jnp.float32))
    return pl.pallas_call(
        functools.partial(solve_kernel, group, lead),
        out_shape=tuple(shapes),
        in_specs=[smem()] + [vmem()] * (len(inputs) - 1),
        out_specs=tuple(vmem() for _ in shapes),
        compiler_params=params(8),
        cost_estimate=pl.CostEstimate(
            flops=8 * tiles * width, bytes_accessed=4 * tiles * width * (len(inputs) + 2), transcendentals=0
        ),
        name="solve",
    )(*inputs)


def update_kernel(here_ref, v_ref, x_ref, *refs):
    out_ref = refs[-1]
    width, span = out_ref.shape
    step = pl.program_id(0)
    masks = piece_masks(here_ref[1] % 2)
    for part in range(span // BLOCK):
        block = step * (span // BLOCK) + part
        coefs = jnp.concatenate([ref[pl.ds(block * 8, 8), :] for ref in refs[: 2 * GROUPS]], axis=0)
        c_high, c_low = split(coefs)
        w_high, w_low = split(pieces(masks, v_ref, block))
        change = lax.dot_general(
            jnp.concatenate([c_high, c_high, c_low], axis=0),
            jnp.concatenate([w_high, w_low, w_high], axis=0),
            (((0,), (0,)), ((), ())),
            preferred_element_type=jnp.float32,
        )
        out_ref[:, part * BLOCK : (part + 1) * BLOCK] = x_ref[:, pl.ds(block * BLOCK, BLOCK)] - change


def update(here, v, slab, coefs, result, chunk, columns):
    width = slab.shape[0]
    span = min(SPAN, slab.shape[1])
    ordered = [c[0] for c in coefs] + [c[1] for c in coefs]
    inputs = [here, v, slab] + ordered
    specs = [smem()] + [vmem()] * (len(inputs) - 1)
    alias = {}
    if result is not None:
        alias = {len(inputs): 0}
        inputs.append(result)
        specs.append(pl.BlockSpec(memory_space=pl.ANY))
    return pl.pallas_call(
        update_kernel,
        grid=(slab.shape[1] // span,),
        out_shape=jax.ShapeDtypeStruct((columns, slab.shape[1]), jnp.float32),
        in_specs=specs,
        out_specs=pl.BlockSpec((width, span), lambda b: (chunk, b)),
        input_output_aliases=alias,
        compiler_params=params(14),
        cost_estimate=pl.CostEstimate(
            flops=2 * 192 * width * slab.shape[1], bytes_accessed=8 * width * slab.shape[1], transcendentals=0
        ),
        name="update",
    )(*inputs)


def shards(slab, stored, owner):
    parts = lax.axis_size("row")
    columns, rows = slab.shape
    tiles = rows // BAND
    width = columns // CHUNKS
    here = jnp.stack([lax.axis_index("col"), lax.axis_index("row"), jnp.int32(parts)]).astype(jnp.int32)
    held = [load(slab, chunk, width) for chunk in range(CHUNKS)]
    keep, other = fetch_vectors(here, stored, owner)
    v, table, norms = make_table(here, keep, other)
    if tiles < width:
        norms = jnp.pad(norms, ((0, 0), (0, 0), (0, width - tiles)))
    norms = norms.reshape(2, 8, -1, width).transpose(2, 0, 1, 3)
    own, rest, coefs = [], [], [[] for _ in range(CHUNKS)]
    for chunk in range(CHUNKS):
        one, two, more = products(here, v, held[chunk], norms, chunk)
        own.append((one, two))
        rest.append(more)
    tau = None
    for group in range(GROUPS):
        for chunk in range(CHUNKS):
            got = (swap_first(own[chunk][0]), swap_second(own[chunk][1]))
            outs = solve(here, table, tau, own[chunk], got, rest[chunk], coefs[chunk], group)
            coefs[chunk].append(outs[:2])
            if group < GROUPS - 1:
                own[chunk] = outs[2:4]
            if tau is None:
                tau = outs[-1]
    result = None
    for chunk in range(CHUNKS):
        result = update(here, v, held[chunk], coefs[chunk], result, chunk, columns)
    return result


def solution(mesh):
    placed = (P("col", "row"), P(("row", "col"), None), P())
    return jax.shard_map(
        shards, mesh=mesh, in_specs=placed, out_specs=P("col", "row"), check_vma=False
    )
```

```python
import functools

import jax
import jax.numpy as jnp
import numpy as np
from jax import lax
from jax.experimental import pallas as pl
from jax.experimental.pallas import tpu as pltpu
from jax.sharding import PartitionSpec as P

BAND = 64
GROUPS = 4
LANES = 128
BLOCK = 8 * BAND
LOADS = 8
STEP = 1 << 18
SLOTS = 4
MIB = 1 << 20
HIGH = lax.Precision.HIGHEST
PAIRS = [(g, h) for g in range(GROUPS) for h in range(g)]


def offset_of(group):
    return 1 + (37 * group + 11) % 63


def swap(block, axis, bit):
    size = lax.axis_size(axis)
    return lax.ppermute(block, axis, [(i, i ^ bit) for i in range(size)])


def swap_first(block):
    return swap(block, "row", 1)


def swap_second(block):
    size = lax.axis_size("row")
    route = [(i, (i + 1) % size if i % 2 else (i - 1) % size) for i in range(size)]
    return lax.ppermute(block, "row", route)


def params(mib):
    return pltpu.CompilerParams(vmem_limit_bytes=mib * MIB)


def vmem():
    return pl.BlockSpec(memory_space=pltpu.VMEM)


def smem():
    return pl.BlockSpec(memory_space=pltpu.SMEM)


def deal_kernel(parts, here_ref, row_ref, *out_refs):
    pairs = out_refs[0].shape[0]
    lane = lax.broadcasted_iota(jnp.int32, (pairs, LANES), 1)
    for s, out_ref in enumerate(out_refs):
        to = here_ref[1] ^ s
        one = row_ref[pl.ds(to // 2, pairs, stride=parts), :]
        two = row_ref[pl.ds(to // 2 + parts // 2, pairs, stride=parts), :]
        even = jnp.where(lane < BAND, one, pltpu.roll(two, BAND, 1))
        odd = jnp.where(lane < BAND, pltpu.roll(one, BAND, 1), two)
        out_ref[...] = jnp.where(to % 2 == 0, even, odd)


def deal(here, row, parts):
    pairs = row.shape[0] // parts
    shape = jax.ShapeDtypeStruct((pairs, LANES), jnp.float32)
    return pl.pallas_call(
        functools.partial(deal_kernel, parts),
        out_shape=(shape,) * parts,
        in_specs=[smem(), vmem()],
        out_specs=(vmem(),) * parts,
        compiler_params=params(6),
        name="deal",
    )(here, row)


def pick_kernel(n_col, parts, here_ref, owner_ref, *refs):
    keep_ref, give_ref = refs[-2:]
    half = keep_ref.shape[1]
    col, row = here_ref[0], here_ref[1]
    core = col % 2
    keep_ref[...] = jnp.zeros(keep_ref.shape, jnp.float32)
    give_ref[...] = jnp.zeros(give_ref.shape, jnp.float32)
    for g in range(GROUPS):
        owner = owner_ref[g]
        for s, got_ref in zip(reversed(range(parts)), refs[:parts]):

            @pl.when((owner % n_col == col) & (owner // n_col == row ^ s))
            def _():
                keep_ref[g] = got_ref[pl.ds(core * half, half), :]
                give_ref[g] = got_ref[pl.ds((1 - core) * half, half), :]


def pick(here, owner, got, tokens, n_col):
    half = got[0].shape[0] // 2
    shape = jax.ShapeDtypeStruct((GROUPS, half, LANES), jnp.float32)
    return pl.pallas_call(
        functools.partial(pick_kernel, n_col, len(got)),
        out_shape=(shape, shape),
        in_specs=[smem(), smem()] + [vmem()] * (len(got) + len(tokens)),
        out_specs=(vmem(), vmem()),
        compiler_params=params(6),
        name="pick",
    )(here, owner, *got, *tokens)


def fetch_vectors(here, owner, stored, slab, width):
    parts, n_col = lax.axis_size("row"), lax.axis_size("col")
    rows = deal(here, stored.reshape(-1, LANES), parts)
    got = [swap(rows[s], "row", s) for s in reversed(range(1, parts))] + [rows[0]]
    half = width // 2
    held, token = load(slab, 0, half, width)
    keep, give = pick(here, owner, got, [token], n_col)
    keep = keep + swap(give, "col", 1)
    held, token = load(slab, half, width - half, width, held, keep)
    bit = 2
    while bit < n_col:
        keep = keep + swap(keep, "col", bit) + token
        bit *= 2
    return keep, swap(keep, "col", 1), held


def first_lanes(parity, group, lane):
    return jnp.where(lane >= offset_of(group), 1, 0) != parity


def spread(pairs, tiles_ref):
    half = pairs.shape[0]
    tiles_ref[pl.ds(0, half, stride=2), :] = pairs
    tiles_ref[pl.ds(1, half, stride=2), :] = pltpu.roll(pairs, BAND, 1)
    return tiles_ref[...]


def lane_grid():
    lane = lax.broadcasted_iota(jnp.int32, (LANES, LANES), 0)
    col = lax.broadcasted_iota(jnp.int32, (LANES, LANES), 1)
    return lane, col


def sum_into(product, hit):
    ones = jnp.where(hit, 1.0, 0.0).astype(jnp.float32)
    return jnp.dot(product, ones, precision=HIGH, preferred_element_type=jnp.float32)


def collect_kernel(here_ref, keep_ref, other_ref, v_ref, sums_ref, norms_ref, tiles_ref):
    half = keep_ref.shape[1]
    core, parity = here_ref[0] % 2, here_ref[1] % 2
    lane, col = lane_grid()
    sums = jnp.zeros(sums_ref.shape, jnp.float32)
    for g in range(GROUPS):
        v_ref[g, pl.ds(core * half, half), :] = keep_ref[g]
        v_ref[g, pl.ds((1 - core) * half, half), :] = other_ref[g]
        tiles = spread(v_ref[g], tiles_ref.at[g])
        spot = jnp.where(first_lanes(parity, g, lane), g, GROUPS + g)
        sums += sum_into(tiles * tiles, (lane < BAND) & (col == spot))
    sums_ref[...] = sums
    turned = jnp.transpose(sums)[:8]
    norms_ref[0] = turned
    norms_ref[1] = pltpu.roll(turned, GROUPS, 0)


def collect(here, keep, other):
    _, half, _ = keep.shape
    tiles = 4 * half
    return pl.pallas_call(
        collect_kernel,
        out_shape=(
            jax.ShapeDtypeStruct((GROUPS, 2 * half, LANES), jnp.float32),
            jax.ShapeDtypeStruct((tiles, LANES), jnp.float32),
            jax.ShapeDtypeStruct((2, 8, tiles), jnp.float32),
        ),
        in_specs=[smem(), vmem(), vmem()],
        out_specs=(vmem(), vmem(), vmem()),
        scratch_shapes=[pltpu.VMEM((GROUPS, tiles, LANES), jnp.float32)],
        compiler_params=params(6),
        name="collect",
    )(here, keep, other)


def table_kernel(here_ref, v_ref, token_ref, table_ref, tiles_ref):
    parity = here_ref[1] % 2
    lane, col = lane_grid()
    first = [first_lanes(parity, g, lane) for g in range(GROUPS)]
    tiles = [spread(v_ref[g], tiles_ref.at[g]) for g in range(GROUPS)]
    table = jnp.zeros(table_ref.shape, jnp.float32)
    for at, (g, h) in enumerate(PAIRS):
        spot = 4 * at + jnp.where(first[g], 0, 2) + jnp.where(first[h], 0, 1)
        table += sum_into(tiles[g] * tiles[h], (lane < BAND) & (col == spot))
    table_ref[...] = table


def make_table(here, v, token):
    tiles = 2 * v.shape[1]
    return pl.pallas_call(
        table_kernel,
        out_shape=jax.ShapeDtypeStruct((tiles, LANES), jnp.float32),
        in_specs=[smem(), vmem(), pl.BlockSpec(memory_space=pl.ANY)],
        out_specs=vmem(),
        scratch_shapes=[pltpu.VMEM((GROUPS, tiles, LANES), jnp.float32)],
        compiler_params=params(6),
        name="table",
    )(here, v, token)


def load_kernel(start, width, x_ref, *refs):
    out_ref, token_ref, sems = refs[-3:]
    rows = width // LOADS
    first = out_ref.shape[0] - width if len(refs) > 3 else 0
    copies = [
        pltpu.make_async_copy(
            x_ref.at[pl.ds(start + i * rows, rows)], out_ref.at[pl.ds(first + i * rows, rows)], sems.at[i]
        )
        for i in range(LOADS)
    ]
    for copy in copies:
        copy.start()
    token_ref[...] = jnp.zeros(token_ref.shape, jnp.float32)
    for copy in copies:
        copy.wait()


def load(slab, start, width, total, into=None, after=None):
    given = [] if into is None else [into, after]
    return pl.pallas_call(
        functools.partial(load_kernel, start, width),
        out_shape=(
            jax.ShapeDtypeStruct((total, slab.shape[1]), slab.dtype),
            jax.ShapeDtypeStruct((8, LANES) if after is None else after.shape, jnp.float32),
        ),
        in_specs=[pl.BlockSpec(memory_space=pltpu.HBM)]
        + [vmem(), pl.BlockSpec(memory_space=pl.ANY)][: len(given)],
        out_specs=(vmem(), vmem()),
        scratch_shapes=[pltpu.SemaphoreType.DMA((LOADS,))],
        input_output_aliases={1: 0} if given else {},
        compiler_params=params(6),
        cost_estimate=pl.CostEstimate(flops=0, bytes_accessed=8 * width * slab.shape[1], transcendentals=0),
        name="load",
    )(slab, *given)


def piece_masks(parity):
    lane = lax.broadcasted_iota(jnp.int32, (8, BLOCK), 1)
    tile = lax.broadcasted_iota(jnp.int32, (8, BLOCK), 0)
    own = lane // BAND == tile
    hits = [first_lanes(parity, g, lane % BAND) for g in range(GROUPS)]
    first = [jnp.where(own & hit, 1.0, 0.0).astype(jnp.float32) for hit in hits]
    second = [jnp.where(own & jnp.logical_not(hit), 1.0, 0.0).astype(jnp.float32) for hit in hits]
    return first, second


def pieces(masks, v_ref, block):
    rows = BLOCK // LANES
    wide = [
        jnp.concatenate(
            [jnp.broadcast_to(v_ref[g, pl.ds(rows * block + j, 1), :], (8, LANES)) for j in range(rows)], axis=1
        )
        for g in range(GROUPS)
    ]
    return jnp.concatenate([m * w for kind in masks for m, w in zip(kind, wide)], axis=0)


def split(x):
    high = x.astype(jnp.bfloat16)
    return high, (x - high.astype(jnp.float32)).astype(jnp.bfloat16)


def products_kernel(start, here_ref, v_ref, x_ref, *refs):
    if start is None:
        held_ref = x_ref
        norms_ref, one_ref, two_ref, rest_ref, weights_ref = refs
        masks = piece_masks(here_ref[1] % 2)
    else:
        weights_ref, one_ref, two_ref, rest_ref, held_ref, sems = refs
    width, columns = held_ref.shape
    tiles = columns // BAND
    slices = 1 if start is None else LOADS
    span = columns // slices
    copies = []
    if start is not None:
        copies = [
            pltpu.make_async_copy(
                x_ref.at[pl.ds(start, width), pl.ds(i * span, span)],
                held_ref.at[:, pl.ds(i * span, span)],
                sems.at[i],
            )
            for i in range(slices)
        ]
    for copy in copies:
        copy.start()

    def step(block):
        if start is None:
            w_both = jnp.concatenate(split(pieces(masks, v_ref, block)), axis=0)
            weights_ref[block] = w_both
        else:
            w_both = weights_ref[block]
        x_high, x_low = split(held_ref[:, pl.ds(block * BLOCK, BLOCK)])
        across = (((1,), (1,)), ((), ()))
        if width <= LANES:
            both = lax.dot_general(
                w_both, jnp.concatenate([x_high, x_low], axis=0), across, preferred_element_type=jnp.float32
            )
            sums = both[:64, :width] + (both[64:, :width] + both[:64, width:])
        else:
            both = lax.dot_general(w_both, x_high, across, preferred_element_type=jnp.float32)
            low = lax.dot_general(w_both[:64], x_low, across, preferred_element_type=jnp.float32)
            sums = both[:64] + both[64:] + low
        spot = pl.ds(block * 8, 8)
        one_ref[spot, :] = sums[0:8]
        two_ref[spot, :] = sums[32:40]
        for g in range(1, GROUPS):
            rest_ref[g - 1, spot, :] = sums[8 * g : 8 * g + 8]
            rest_ref[g + 2, spot, :] = sums[32 + 8 * g : 40 + 8 * g]

    blocks = span // BLOCK
    for i in range(slices):
        if copies:
            copies[i].wait()
        pl.loop(i * blocks, (i + 1) * blocks, unroll=min(blocks, 8))(step)

    if start is None:
        for at in range(norms_ref.shape[0]):
            one_ref[tiles + 8 * at : tiles + 8 * at + 8] = norms_ref[at, 0]
            two_ref[tiles + 8 * at : tiles + 8 * at + 8] = norms_ref[at, 1]


def products(here, v, x, more, start=None, width=None):
    width, tiles = width or x.shape[0], x.shape[1] // BAND
    extra = 8 * more.shape[0] if start is None else 0
    message = jax.ShapeDtypeStruct((tiles + extra, width), jnp.float32)
    shapes = [message, message, jax.ShapeDtypeStruct((2 * GROUPS - 2, tiles, width), jnp.float32)]
    specs = [smem()] + [vmem()] * 3
    scratch = []
    if start is None:
        shapes.append(jax.ShapeDtypeStruct((tiles // 8, 128, BLOCK), jnp.bfloat16))
    else:
        specs[2] = pl.BlockSpec(memory_space=pltpu.HBM)
        shapes.append(jax.ShapeDtypeStruct((width, x.shape[1]), jnp.float32))
        scratch.append(pltpu.SemaphoreType.DMA((LOADS,)))
    return pl.pallas_call(
        functools.partial(products_kernel, start),
        out_shape=tuple(shapes),
        in_specs=specs,
        out_specs=(vmem(),) * len(shapes),
        scratch_shapes=scratch,
        compiler_params=params(6),
        cost_estimate=pl.CostEstimate(
            flops=2 * 192 * width * x.shape[1], bytes_accessed=4 * width * x.shape[1], transcendentals=0
        ),
        name="products",
    )(here, v, x, more)


def align(x, here_ref):
    back = jnp.concatenate([x[1:], x[:1]], axis=0)
    on = jnp.concatenate([x[-1:], x[:-1]], axis=0)
    return jnp.where(here_ref[1] == 0, on, jnp.where(here_ref[1] == here_ref[2] - 1, back, x))


def scales_of(here_ref, sums_ref, got_one_ref, got_two_ref):
    tiles = sums_ref.shape[0]
    got = []
    for ref in (got_one_ref, got_two_ref):
        rows = [ref[at : at + 8, :] for at in range(tiles, ref.shape[0], 8)]
        rows = jnp.concatenate(rows, axis=1)[:, :tiles]
        got.append(jnp.transpose(jnp.concatenate([rows] + [jnp.zeros_like(rows)] * (LANES // 8 - 1), axis=0)))
    row = lax.broadcasted_iota(jnp.int32, (tiles, LANES), 0)
    gone = ((here_ref[1] == 0) & (row == 0)) | ((here_ref[1] == here_ref[2] - 1) & (row == tiles - 1))
    col = lax.broadcasted_iota(jnp.int32, (tiles, LANES), 1)
    other = jnp.where(col < GROUPS, got[0], pltpu.roll(align(got[1], here_ref), GROUPS, 1))
    tau = 2.0 / (sums_ref[...] + other + 1e-6)
    return jnp.where(gone & (col >= GROUPS), 0.0, tau)


def solve_kernel(group, lead, columns, here_ref, table_ref, tau_ref, after_ref, *refs):
    refs = list(refs)
    own_one_ref, own_two_ref, got_one_ref, got_two_ref = [refs.pop(0) for _ in range(4)]
    last = group == GROUPS - 1
    tiles = table_ref.shape[0]
    tau = scales_of(here_ref, tau_ref, got_one_ref, got_two_ref) if lead else tau_ref[...]
    one = tau[:, group : group + 1] * (own_one_ref[:tiles, columns] + got_one_ref[:tiles])
    two = tau[:, GROUPS + group : GROUPS + group + 1] * (
        own_two_ref[:tiles, columns] + align(got_two_ref[:tiles], here_ref)
    )
    if last:
        coef_one_ref, coef_two_ref = refs
        coef_one_ref[...] = one
        coef_two_ref[...] = two
        return
    rest_ref = refs.pop(0)
    before = [refs.pop(0) for _ in range(2 * group)]
    coef_one_ref, coef_two_ref = refs.pop(0), refs.pop(0)
    coef_one_ref[...] = one
    coef_two_ref[...] = two
    if lead:
        refs.pop()[...] = tau
    table = table_ref[...]
    later = group + 1
    next_one = rest_ref[later - 1]
    next_two = rest_ref[later + 2]
    for h in range(later):
        at = 4 * PAIRS.index((later, h))
        c_one, c_two = (one, two) if h == group else (before[2 * h][...], before[2 * h + 1][...])
        next_one = next_one - table[:, at : at + 1] * c_one - table[:, at + 1 : at + 2] * c_two
        next_two = next_two - table[:, at + 2 : at + 3] * c_one - table[:, at + 3 : at + 4] * c_two
    part = refs[0].shape[1]
    for i in range(len(refs) // 2):
        refs[2 * i][...] = next_one[:, i * part : (i + 1) * part]
        refs[2 * i + 1][...] = next_two[:, i * part : (i + 1) * part]


def solve(here, table, tau, own, got, rest, before, group, after, lead=False, columns=None, parts=1):
    tiles, width = table.shape[0], got[0].shape[1]
    columns = columns or slice(0, width)
    last = group == GROUPS - 1
    inputs = [here, table, tau, after] + list(own) + list(got)
    shapes = [jax.ShapeDtypeStruct((tiles, width), jnp.float32)] * 2
    if not last:
        inputs += [rest] + [c for pair in before for c in pair]
        shapes += [jax.ShapeDtypeStruct((tiles, width // parts), jnp.float32)] * (2 * parts)
    if lead:
        shapes.append(jax.ShapeDtypeStruct((tiles, LANES), jnp.float32))
    return pl.pallas_call(
        functools.partial(solve_kernel, group, lead, columns),
        out_shape=tuple(shapes),
        in_specs=[smem(), vmem(), vmem(), pl.BlockSpec(memory_space=pl.ANY)] + [vmem()] * (len(inputs) - 4),
        out_specs=tuple(vmem() for _ in shapes),
        compiler_params=params(6),
        cost_estimate=pl.CostEstimate(flops=tiles, bytes_accessed=4 * tiles, transcendentals=0),
        name="solve",
    )(*inputs)


def update_kernel(start, columns, weights_ref, x_ref, *refs):
    out_ref, token_ref, stage_ref, sems = refs[-4:]
    slots, width, span = stage_ref.shape
    token_ref[...] = jnp.zeros(token_ref.shape, jnp.float32)

    def write(slot, step):
        to = out_ref.at[pl.ds(start, width), pl.ds(step * span, span)]
        return pltpu.make_async_copy(stage_ref.at[slot], to, sems.at[slot])

    for step in range(x_ref.shape[1] // span):
        slot = step % slots
        if step >= slots:
            write(slot, step - slots).wait()
        for part in range(span // BLOCK):
            block = step * (span // BLOCK) + part
            spot = pl.ds(block * 8, 8)
            coefs = [ref[spot, :] if ref.shape[1] == width else ref[spot, columns] for ref in refs[: 2 * GROUPS]]
            c_high, c_low = split(jnp.concatenate(coefs, axis=0))
            w_both = weights_ref[block]
            change = lax.dot_general(
                jnp.concatenate([c_high, c_high, c_low], axis=0),
                jnp.concatenate([w_both, w_both[:64]], axis=0),
                (((0,), (0,)), ((), ())),
                preferred_element_type=jnp.float32,
            )
            here = slice(block * BLOCK, (block + 1) * BLOCK)
            stage_ref[slot, :, part * BLOCK : (part + 1) * BLOCK] = x_ref[columns, here] - change
        write(slot, step).start()
    steps = x_ref.shape[1] // span
    for step in range(max(0, steps - slots), steps):
        write(step % slots, step).wait()


def update(weights, held, coefs, result, start, columns, total):
    width = columns.stop - columns.start
    span = min(STEP // width, held.shape[1])
    inputs = [weights, held] + [c[0] for c in coefs] + [c[1] for c in coefs]
    specs = [vmem()] * len(inputs)
    alias = {}
    if result is not None:
        alias = {len(inputs): 0}
        inputs.append(result)
        specs.append(pl.BlockSpec(memory_space=pl.ANY))
    return pl.pallas_call(
        functools.partial(update_kernel, start + columns.start, columns),
        out_shape=(
            jax.ShapeDtypeStruct((total, held.shape[1]), jnp.float32),
            jax.ShapeDtypeStruct((8, LANES), jnp.float32),
        ),
        in_specs=specs,
        out_specs=(pl.BlockSpec(memory_space=pltpu.HBM), vmem()),
        scratch_shapes=[pltpu.VMEM((SLOTS, width, span), jnp.float32), pltpu.SemaphoreType.DMA((SLOTS,))],
        input_output_aliases=alias,
        compiler_params=params(7),
        cost_estimate=pl.CostEstimate(
            flops=2 * 192 * width * held.shape[1], bytes_accessed=8 * width * held.shape[1], transcendentals=0
        ),
        name="update",
    )(*inputs)


def shards(slab, stored, owner):
    parts = lax.axis_size("row")
    total, rows = slab.shape
    tiles = rows // BAND
    width = total // 2
    here = [lax.axis_index("col"), lax.axis_index("row"), jnp.int32(parts)]
    here = jnp.stack(here).astype(jnp.int32)
    keep, other, held = fetch_vectors(here, owner, stored, slab, width)
    v, sums, norms = collect(here, keep, other)
    if tiles < width:
        norms = jnp.pad(norms, ((0, 0), (0, 0), (0, width - tiles)))
    norms = norms.reshape(2, 8, -1, width).transpose(2, 0, 1, 3)
    first = products(here, v, held, norms)
    weights = first[3]
    second = products(here, v, slab, weights, width, width)
    table = make_table(here, v, second[2])
    held = [held, second[3]]
    own, rest, coefs = [first[:2], second[:2]], [first[2], second[2]], [[], []]
    tau, after = sums, table
    for group in range(GROUPS - 1):
        for i in range(2):
            got = (swap_first(own[i][0]), swap_second(own[i][1]))
            cut = 2 if group == GROUPS - 2 and i == 1 and width % (2 * LANES) == 0 else 1
            lead = group == 0 and i == 0
            outs = solve(here, table, tau, own[i], got, rest[i], coefs[i], group, after, lead, parts=cut)
            coefs[i].append(outs[:2])
            own[i] = outs[2 : 2 + 2 * cut]
            after = outs[0]
            if lead:
                tau = outs[-1]
    result = None
    group = GROUPS - 1
    jobs = [(0, 0, 1, own[0])]
    cut = len(own[1]) // 2
    jobs += [(1, k, cut, own[1][2 * k : 2 * k + 2]) for k in range(cut)]
    for i, k, cut, mine in jobs:
        part = width // cut
        got = (swap_first(mine[0]), swap_second(mine[1]))
        last = solve(here, table, tau, mine, got, None, None, group, after)
        columns = slice(k * part, (k + 1) * part)
        result, after = update(weights, held[i], coefs[i] + [last], result, i * width, columns, total)
    return result


def solution(mesh):
    placed = (P("col", "row"), P(("row", "col"), None), P())
    return jax.shard_map(
        shards, mesh=mesh, in_specs=placed, out_specs=P("col", "row"), check_vma=False
    )
```

```python
import functools

import jax
import jax.numpy as jnp
import numpy as np
from jax import lax
from jax.experimental import pallas as pl
from jax.experimental.pallas import tpu as pltpu
from jax.sharding import PartitionSpec as P

BAND = 64
GROUPS = 4
LANES = 128
BLOCK = 8 * BAND
LOADS = 8
UNROLL = 16
STEP = 1 << 18
SLOTS = 4
MIB = 1 << 20
HIGH = lax.Precision.HIGHEST
PAIRS = [(g, h) for g in range(GROUPS) for h in range(g)]


def offset_of(group):
    return 1 + (37 * group + 11) % 63


def swap(block, axis, bit):
    size = lax.axis_size(axis)
    return lax.ppermute(block, axis, [(i, i ^ bit) for i in range(size)])


def swap_first(block):
    return swap(block, "row", 1)


def swap_second(block):
    size = lax.axis_size("row")
    route = [(i, (i + 1) % size if i % 2 else (i - 1) % size) for i in range(size)]
    return lax.ppermute(block, "row", route)


def params(mib):
    return pltpu.CompilerParams(vmem_limit_bytes=mib * MIB)


def vmem():
    return pl.BlockSpec(memory_space=pltpu.VMEM)


def smem():
    return pl.BlockSpec(memory_space=pltpu.SMEM)


def deal_kernel(parts, here_ref, row_ref, *out_refs):
    pairs = out_refs[0].shape[0]
    lane = lax.broadcasted_iota(jnp.int32, (pairs, LANES), 1)
    for s, out_ref in enumerate(out_refs):
        to = here_ref[1] ^ s
        one = row_ref[pl.ds(to // 2, pairs, stride=parts), :]
        two = row_ref[pl.ds(to // 2 + parts // 2, pairs, stride=parts), :]
        even = jnp.where(lane < BAND, one, pltpu.roll(two, BAND, 1))
        odd = jnp.where(lane < BAND, pltpu.roll(one, BAND, 1), two)
        out_ref[...] = jnp.where(to % 2 == 0, even, odd)


def deal(here, row, parts):
    pairs = row.shape[0] // parts
    shape = jax.ShapeDtypeStruct((pairs, LANES), jnp.float32)
    return pl.pallas_call(
        functools.partial(deal_kernel, parts),
        out_shape=(shape,) * parts,
        in_specs=[smem(), vmem()],
        out_specs=(vmem(),) * parts,
        compiler_params=params(8),
        name="deal",
    )(here, row)


def pick_kernel(n_col, parts, here_ref, owner_ref, *refs):
    keep_ref, give_ref = refs[-2:]
    half = keep_ref.shape[1]
    col, row = here_ref[0], here_ref[1]
    core = col % 2
    keep_ref[...] = jnp.zeros(keep_ref.shape, jnp.float32)
    give_ref[...] = jnp.zeros(give_ref.shape, jnp.float32)
    for g in range(GROUPS):
        owner = owner_ref[g]
        for s, got_ref in zip(reversed(range(parts)), refs[:parts]):

            @pl.when((owner % n_col == col) & (owner // n_col == row ^ s))
            def _():
                keep_ref[g] = got_ref[pl.ds(core * half, half), :]
                give_ref[g] = got_ref[pl.ds((1 - core) * half, half), :]


def pick(here, owner, got, tokens, n_col):
    half = got[0].shape[0] // 2
    shape = jax.ShapeDtypeStruct((GROUPS, half, LANES), jnp.float32)
    return pl.pallas_call(
        functools.partial(pick_kernel, n_col, len(got)),
        out_shape=(shape, shape),
        in_specs=[smem(), smem()] + [vmem()] * (len(got) + len(tokens)),
        out_specs=(vmem(), vmem()),
        compiler_params=params(8),
        name="pick",
    )(here, owner, *got, *tokens)


def fetch_vectors(here, owner, stored, slab, width):
    parts, n_col = lax.axis_size("row"), lax.axis_size("col")
    rows = deal(here, stored.reshape(-1, LANES), parts)
    got = [swap(rows[s], "row", s) for s in reversed(range(1, parts))] + [rows[0]]
    half = width // 2
    held, token = load(slab, 0, half, width)
    keep, give = pick(here, owner, got, [token], n_col)
    keep = keep + swap(give, "col", 1)
    held, token = load(slab, half, width - half, width, held, keep)
    bit = 2
    while bit < n_col:
        keep = keep + swap(keep, "col", bit) + token
        bit *= 2
    return keep, swap(keep, "col", 1), held


def first_lanes(parity, group, lane):
    return jnp.where(lane >= offset_of(group), 1, 0) != parity


def spread(pairs, tiles_ref):
    half = pairs.shape[0]
    tiles_ref[pl.ds(0, half, stride=2), :] = pairs
    tiles_ref[pl.ds(1, half, stride=2), :] = pltpu.roll(pairs, BAND, 1)
    return tiles_ref[...]


def lane_grid():
    lane = lax.broadcasted_iota(jnp.int32, (LANES, LANES), 0)
    col = lax.broadcasted_iota(jnp.int32, (LANES, LANES), 1)
    return lane, col


def sum_into(product, hit):
    ones = jnp.where(hit, 1.0, 0.0).astype(jnp.float32)
    return jnp.dot(product, ones, precision=HIGH, preferred_element_type=jnp.float32)


def collect_kernel(here_ref, keep_ref, other_ref, v_ref, sums_ref, norms_ref, tiles_ref):
    half = keep_ref.shape[1]
    core, parity = here_ref[0] % 2, here_ref[1] % 2
    lane, col = lane_grid()
    sums = jnp.zeros(sums_ref.shape, jnp.float32)
    for g in range(GROUPS):
        v_ref[g, pl.ds(core * half, half), :] = keep_ref[g]
        v_ref[g, pl.ds((1 - core) * half, half), :] = other_ref[g]
        tiles = spread(v_ref[g], tiles_ref.at[g])
        spot = jnp.where(first_lanes(parity, g, lane), g, GROUPS + g)
        sums += sum_into(tiles * tiles, (lane < BAND) & (col == spot))
    sums_ref[...] = sums
    turned = jnp.transpose(sums)[:8]
    norms_ref[0] = turned
    norms_ref[1] = pltpu.roll(turned, GROUPS, 0)


def collect(here, keep, other):
    _, half, _ = keep.shape
    tiles = 4 * half
    return pl.pallas_call(
        collect_kernel,
        out_shape=(
            jax.ShapeDtypeStruct((GROUPS, 2 * half, LANES), jnp.float32),
            jax.ShapeDtypeStruct((tiles, LANES), jnp.float32),
            jax.ShapeDtypeStruct((2, 8, tiles), jnp.float32),
        ),
        in_specs=[smem(), vmem(), vmem()],
        out_specs=(vmem(), vmem(), vmem()),
        scratch_shapes=[pltpu.VMEM((GROUPS, tiles, LANES), jnp.float32)],
        compiler_params=params(8),
        name="collect",
    )(here, keep, other)


def table_kernel(here_ref, v_ref, token_ref, table_ref, tiles_ref):
    parity = here_ref[1] % 2
    lane, col = lane_grid()
    first = [first_lanes(parity, g, lane) for g in range(GROUPS)]
    tiles = [spread(v_ref[g], tiles_ref.at[g]) for g in range(GROUPS)]
    table = jnp.zeros(table_ref.shape, jnp.float32)
    for at, (g, h) in enumerate(PAIRS):
        spot = 4 * at + jnp.where(first[g], 0, 2) + jnp.where(first[h], 0, 1)
        table += sum_into(tiles[g] * tiles[h], (lane < BAND) & (col == spot))
    table_ref[...] = table


def make_table(here, v, token):
    tiles = 2 * v.shape[1]
    return pl.pallas_call(
        table_kernel,
        out_shape=jax.ShapeDtypeStruct((tiles, LANES), jnp.float32),
        in_specs=[smem(), vmem(), pl.BlockSpec(memory_space=pl.ANY)],
        out_specs=vmem(),
        scratch_shapes=[pltpu.VMEM((GROUPS, tiles, LANES), jnp.float32)],
        compiler_params=params(8),
        name="table",
    )(here, v, token)


def load_kernel(start, width, x_ref, *refs):
    out_ref, token_ref, sems = refs[-3:]
    rows = width // LOADS
    first = out_ref.shape[0] - width if len(refs) > 3 else 0
    copies = [
        pltpu.make_async_copy(
            x_ref.at[pl.ds(start + i * rows, rows)], out_ref.at[pl.ds(first + i * rows, rows)], sems.at[i]
        )
        for i in range(LOADS)
    ]
    for copy in copies:
        copy.start()
    token_ref[...] = jnp.zeros(token_ref.shape, jnp.float32)
    for copy in copies:
        copy.wait()


def load(slab, start, width, total, into=None, after=None):
    given = [] if into is None else [into, after]
    return pl.pallas_call(
        functools.partial(load_kernel, start, width),
        out_shape=(
            jax.ShapeDtypeStruct((total, slab.shape[1]), slab.dtype),
            jax.ShapeDtypeStruct((8, LANES) if after is None else after.shape, jnp.float32),
        ),
        in_specs=[pl.BlockSpec(memory_space=pltpu.HBM)]
        + [vmem(), pl.BlockSpec(memory_space=pl.ANY)][: len(given)],
        out_specs=(vmem(), vmem()),
        scratch_shapes=[pltpu.SemaphoreType.DMA((LOADS,))],
        input_output_aliases={1: 0} if given else {},
        compiler_params=params(8),
        cost_estimate=pl.CostEstimate(flops=0, bytes_accessed=8 * width * slab.shape[1], transcendentals=0),
        name="load",
    )(slab, *given)


def piece_masks(parity):
    lane = lax.broadcasted_iota(jnp.int32, (8, BLOCK), 1)
    tile = lax.broadcasted_iota(jnp.int32, (8, BLOCK), 0)
    own = lane // BAND == tile
    hits = [first_lanes(parity, g, lane % BAND) for g in range(GROUPS)]
    first = [jnp.where(own & hit, 1.0, 0.0).astype(jnp.float32) for hit in hits]
    second = [jnp.where(own & jnp.logical_not(hit), 1.0, 0.0).astype(jnp.float32) for hit in hits]
    return first, second


def pieces(masks, v_ref, block):
    rows = BLOCK // LANES
    wide = [
        jnp.concatenate(
            [jnp.broadcast_to(v_ref[g, pl.ds(rows * block + j, 1), :], (8, LANES)) for j in range(rows)], axis=1
        )
        for g in range(GROUPS)
    ]
    return jnp.concatenate([m * w for kind in masks for m, w in zip(kind, wide)], axis=0)


def split(x):
    high = x.astype(jnp.bfloat16)
    return high, (x - high.astype(jnp.float32)).astype(jnp.bfloat16)


def products_kernel(lead, start, *refs):
    if lead:
        here_ref, v_ref, held_ref, norms_ref, slab_ref = refs[:5]
        one_ref, two_ref, rest_ref, weights_ref, next_ref, sems = refs[5:]
        masks = piece_masks(here_ref[1] % 2)
        rows = next_ref.shape[0] // LOADS
        copies = [
            pltpu.make_async_copy(
                slab_ref.at[pl.ds(start + i * rows, rows)], next_ref.at[pl.ds(i * rows, rows)], sems.at[i]
            )
            for i in range(LOADS)
        ]
        for copy in copies:
            copy.start()
    else:
        held_ref, weights_ref, one_ref, two_ref, rest_ref = refs
    width, columns = held_ref.shape
    tiles = columns // BAND

    def step(block):
        if lead:
            w_both = jnp.concatenate(split(pieces(masks, v_ref, block)), axis=0)
            weights_ref[block] = w_both
        else:
            w_both = weights_ref[block]
        x_high, x_low = split(held_ref[:, pl.ds(block * BLOCK, BLOCK)])
        across = (((1,), (1,)), ((), ()))
        if width <= LANES:
            both = lax.dot_general(
                w_both, jnp.concatenate([x_high, x_low], axis=0), across, preferred_element_type=jnp.float32
            )
            sums = both[:64, :width] + (both[64:, :width] + both[:64, width:])
        else:
            both = lax.dot_general(w_both, x_high, across, preferred_element_type=jnp.float32)
            low = lax.dot_general(w_both[:64], x_low, across, preferred_element_type=jnp.float32)
            sums = both[:64] + both[64:] + low
        spot = pl.ds(block * 8, 8)
        one_ref[spot, :] = sums[0:8]
        two_ref[spot, :] = sums[32:40]
        for g in range(1, GROUPS):
            rest_ref[g - 1, spot, :] = sums[8 * g : 8 * g + 8]
            rest_ref[g + 2, spot, :] = sums[32 + 8 * g : 40 + 8 * g]

    blocks = columns // BLOCK
    pl.loop(0, blocks, unroll=min(blocks, UNROLL))(step)
    if lead:
        for at in range(norms_ref.shape[0]):
            one_ref[tiles + 8 * at : tiles + 8 * at + 8] = norms_ref[at, 0]
            two_ref[tiles + 8 * at : tiles + 8 * at + 8] = norms_ref[at, 1]
        for copy in copies:
            copy.wait()


def products(inputs, held, extra=0, start=None, rows=None):
    width, tiles = held.shape[0], held.shape[1] // BAND
    lead = start is not None
    message = jax.ShapeDtypeStruct((tiles + extra, width), jnp.float32)
    shapes = [message, message, jax.ShapeDtypeStruct((2 * GROUPS - 2, tiles, width), jnp.float32)]
    specs = [vmem()] * len(inputs)
    if lead:
        shapes.append(jax.ShapeDtypeStruct((tiles // 8, 128, BLOCK), jnp.bfloat16))
        shapes.append(jax.ShapeDtypeStruct((rows, held.shape[1]), jnp.float32))
        specs = [smem(), vmem(), vmem(), vmem(), pl.BlockSpec(memory_space=pltpu.HBM)]
    return pl.pallas_call(
        functools.partial(products_kernel, lead, start),
        out_shape=tuple(shapes),
        in_specs=specs,
        out_specs=(vmem(),) * len(shapes),
        scratch_shapes=[pltpu.SemaphoreType.DMA((LOADS,))] if lead else [],
        compiler_params=params(8),
        cost_estimate=pl.CostEstimate(
            flops=2 * 192 * width * held.shape[1], bytes_accessed=4 * width * held.shape[1], transcendentals=0
        ),
        name="products",
    )(*inputs)


def align(x, here_ref):
    back = jnp.concatenate([x[1:], x[:1]], axis=0)
    on = jnp.concatenate([x[-1:], x[:-1]], axis=0)
    return jnp.where(here_ref[1] == 0, on, jnp.where(here_ref[1] == here_ref[2] - 1, back, x))


def scales_of(here_ref, sums_ref, got_one_ref, got_two_ref):
    tiles = sums_ref.shape[0]
    got = []
    for ref in (got_one_ref, got_two_ref):
        rows = [ref[at : at + 8, :] for at in range(tiles, ref.shape[0], 8)]
        rows = jnp.concatenate(rows, axis=1)[:, :tiles]
        got.append(jnp.transpose(jnp.concatenate([rows] + [jnp.zeros_like(rows)] * (LANES // 8 - 1), axis=0)))
    row = lax.broadcasted_iota(jnp.int32, (tiles, LANES), 0)
    gone = ((here_ref[1] == 0) & (row == 0)) | ((here_ref[1] == here_ref[2] - 1) & (row == tiles - 1))
    col = lax.broadcasted_iota(jnp.int32, (tiles, LANES), 1)
    other = jnp.where(col < GROUPS, got[0], pltpu.roll(align(got[1], here_ref), GROUPS, 1))
    tau = 2.0 / (sums_ref[...] + other + 1e-6)
    return jnp.where(gone & (col >= GROUPS), 0.0, tau)


def solve_kernel(group, lead, here_ref, table_ref, tau_ref, after_ref, *refs):
    refs = list(refs)
    own_one_ref, own_two_ref, got_one_ref, got_two_ref = [refs.pop(0) for _ in range(4)]
    last = group == GROUPS - 1
    tiles = table_ref.shape[0]
    tau = scales_of(here_ref, tau_ref, got_one_ref, got_two_ref) if lead else tau_ref[...]
    one = tau[:, group : group + 1] * (own_one_ref[:tiles] + got_one_ref[:tiles])
    two = tau[:, GROUPS + group : GROUPS + group + 1] * (
        own_two_ref[:tiles] + align(got_two_ref[:tiles], here_ref)
    )
    if last:
        coef_one_ref, coef_two_ref = refs
        coef_one_ref[...] = one
        coef_two_ref[...] = two
        return
    rest_ref = refs.pop(0)
    before = [refs.pop(0) for _ in range(2 * group)]
    coef_one_ref, coef_two_ref = refs.pop(0), refs.pop(0)
    coef_one_ref[...] = one
    coef_two_ref[...] = two
    if lead:
        refs.pop()[...] = tau
    table = table_ref[...]
    later = group + 1
    next_one = rest_ref[later - 1]
    next_two = rest_ref[later + 2]
    for h in range(later):
        at = 4 * PAIRS.index((later, h))
        c_one, c_two = (one, two) if h == group else (before[2 * h][...], before[2 * h + 1][...])
        next_one = next_one - table[:, at : at + 1] * c_one - table[:, at + 1 : at + 2] * c_two
        next_two = next_two - table[:, at + 2 : at + 3] * c_one - table[:, at + 3 : at + 4] * c_two
    refs[0][...] = next_one
    refs[1][...] = next_two


def solve(here, table, tau, own, got, rest, before, group, after, lead=False):
    tiles, width = table.shape[0], got[0].shape[1]
    last = group == GROUPS - 1
    inputs = [here, table, tau, after] + list(own) + list(got)
    shapes = [jax.ShapeDtypeStruct((tiles, width), jnp.float32)] * 2
    if not last:
        inputs += [rest] + [c for pair in before for c in pair]
        shapes += [jax.ShapeDtypeStruct((tiles, width), jnp.float32)] * 2
    if lead:
        shapes.append(jax.ShapeDtypeStruct((tiles, LANES), jnp.float32))
    return pl.pallas_call(
        functools.partial(solve_kernel, group, lead),
        out_shape=tuple(shapes),
        in_specs=[smem(), vmem(), vmem(), pl.BlockSpec(memory_space=pl.ANY)] + [vmem()] * (len(inputs) - 4),
        out_specs=tuple(vmem() for _ in shapes),
        compiler_params=params(8),
        cost_estimate=pl.CostEstimate(flops=tiles, bytes_accessed=4 * tiles, transcendentals=0),
        name="solve",
    )(*inputs)


def update_kernel(start, weights_ref, x_ref, *refs):
    out_ref, token_ref, stage_ref, sems = refs[-4:]
    slots, width, span = stage_ref.shape
    token_ref[...] = jnp.zeros(token_ref.shape, jnp.float32)

    def write(slot, step):
        to = out_ref.at[pl.ds(start, width), pl.ds(step * span, span)]
        return pltpu.make_async_copy(stage_ref.at[slot], to, sems.at[slot])

    for step in range(x_ref.shape[1] // span):
        slot = step % slots
        if step >= slots:
            write(slot, step - slots).wait()
        for part in range(span // BLOCK):
            block = step * (span // BLOCK) + part
            spot = pl.ds(block * 8, 8)
            c_high, c_low = split(jnp.concatenate([ref[spot, :] for ref in refs[: 2 * GROUPS]], axis=0))
            w_both = weights_ref[block]
            change = lax.dot_general(
                jnp.concatenate([c_high, c_high, c_low], axis=0),
                jnp.concatenate([w_both, w_both[:64]], axis=0),
                (((0,), (0,)), ((), ())),
                preferred_element_type=jnp.float32,
            )
            here = slice(block * BLOCK, (block + 1) * BLOCK)
            stage_ref[slot, :, part * BLOCK : (part + 1) * BLOCK] = x_ref[:, here] - change
        write(slot, step).start()
    steps = x_ref.shape[1] // span
    for step in range(max(0, steps - slots), steps):
        write(step % slots, step).wait()


def update(weights, held, coefs, result, start, total):
    width = held.shape[0]
    span = min(STEP // width, held.shape[1])
    inputs = [weights, held] + [c[0] for c in coefs] + [c[1] for c in coefs]
    specs = [vmem()] * len(inputs)
    alias = {}
    if result is not None:
        alias = {len(inputs): 0}
        inputs.append(result)
        specs.append(pl.BlockSpec(memory_space=pl.ANY))
    return pl.pallas_call(
        functools.partial(update_kernel, start),
        out_shape=(
            jax.ShapeDtypeStruct((total, held.shape[1]), jnp.float32),
            jax.ShapeDtypeStruct((8, LANES), jnp.float32),
        ),
        in_specs=specs,
        out_specs=(pl.BlockSpec(memory_space=pltpu.HBM), vmem()),
        scratch_shapes=[pltpu.VMEM((SLOTS, width, span), jnp.float32), pltpu.SemaphoreType.DMA((SLOTS,))],
        input_output_aliases=alias,
        compiler_params=params(8),
        cost_estimate=pl.CostEstimate(
            flops=2 * 192 * width * held.shape[1], bytes_accessed=8 * width * held.shape[1], transcendentals=0
        ),
        name="update",
    )(*inputs)


def shards(slab, stored, owner):
    parts = lax.axis_size("row")
    total, rows = slab.shape
    tiles = rows // BAND
    width = total // 2
    here = [lax.axis_index("col"), lax.axis_index("row"), jnp.int32(parts)]
    here = jnp.stack(here).astype(jnp.int32)
    keep, other, held = fetch_vectors(here, owner, stored, slab, width)
    v, sums, norms = collect(here, keep, other)
    if tiles < width:
        norms = jnp.pad(norms, ((0, 0), (0, 0), (0, width - tiles)))
    norms = norms.reshape(2, 8, -1, width).transpose(2, 0, 1, 3)
    first = products([here, v, held, norms, slab], held, 8 * norms.shape[0], width, total - width)
    weights = first[3]
    held = [held, first[4]]
    second = products([held[1], weights], held[1])
    table = make_table(here, v, second[2])
    own, rest, coefs = [first[:2], second[:2]], [first[2], second[2]], [[], []]
    tau, after = sums, table
    for group in range(GROUPS - 1):
        for i in range(2):
            got = (swap_first(own[i][0]), swap_second(own[i][1]))
            lead = group == 0 and i == 0
            outs = solve(here, table, tau, own[i], got, rest[i], coefs[i], group, after, lead)
            coefs[i].append(outs[:2])
            own[i] = outs[2:4]
            after = outs[0]
            if lead:
                tau = outs[-1]
    result = None
    group = GROUPS - 1
    for i in range(2):
        got = (swap_first(own[i][0]), swap_second(own[i][1]))
        last = solve(here, table, tau, own[i], got, None, None, group, after)
        result, after = update(weights, held[i], coefs[i] + [last], result, i * width, total)
    return result


def solution(mesh):
    placed = (P("col", "row"), P(("row", "col"), None), P())
    return jax.shard_map(
        shards, mesh=mesh, in_specs=placed, out_specs=P("col", "row"), check_vma=False
    )
```

```python
import functools

import jax
import jax.numpy as jnp
import numpy as np
from jax import lax
from jax.experimental import pallas as pl
from jax.experimental.pallas import tpu as pltpu
from jax.sharding import PartitionSpec as P

BAND = 64
GROUPS = 4
LANES = 128
BLOCK = 8 * BAND
LOADS = 2
UNROLL = 16
STEP = 1 << 18
SLOTS = 6
MIB = 1 << 20
HIGH = lax.Precision.HIGHEST
PAIRS = [(g, h) for g in range(GROUPS) for h in range(g)]


def offset_of(group):
    return 1 + (37 * group + 11) % 63


def swap(block, axis, bit):
    size = lax.axis_size(axis)
    return lax.ppermute(block, axis, [(i, i ^ bit) for i in range(size)])


def swap_first(block):
    return swap(block, "row", 1)


def swap_second(block):
    size = lax.axis_size("row")
    route = [(i, (i + 1) % size if i % 2 else (i - 1) % size) for i in range(size)]
    return lax.ppermute(block, "row", route)


def params(mib):
    return pltpu.CompilerParams(vmem_limit_bytes=mib * MIB)


def vmem():
    return pl.BlockSpec(memory_space=pltpu.VMEM)


def smem():
    return pl.BlockSpec(memory_space=pltpu.SMEM)


def deal_kernel(parts, here_ref, row_ref, *out_refs):
    pairs = out_refs[0].shape[0]
    lane = lax.broadcasted_iota(jnp.int32, (pairs, LANES), 1)
    for s, out_ref in enumerate(out_refs):
        to = here_ref[1] ^ s
        one = row_ref[pl.ds(to // 2, pairs, stride=parts), :]
        two = row_ref[pl.ds(to // 2 + parts // 2, pairs, stride=parts), :]
        even = jnp.where(lane < BAND, one, pltpu.roll(two, BAND, 1))
        odd = jnp.where(lane < BAND, pltpu.roll(one, BAND, 1), two)
        out_ref[...] = jnp.where(to % 2 == 0, even, odd)


def deal(here, row, parts):
    pairs = row.shape[0] // parts
    shape = jax.ShapeDtypeStruct((pairs, LANES), jnp.float32)
    return pl.pallas_call(
        functools.partial(deal_kernel, parts),
        out_shape=(shape,) * parts,
        in_specs=[smem(), vmem()],
        out_specs=(vmem(),) * parts,
        compiler_params=params(8),
        name="deal",
    )(here, row)


def pick_kernel(n_col, parts, here_ref, owner_ref, *refs):
    keep_ref, give_ref = refs[-2:]
    half = keep_ref.shape[1]
    col, row = here_ref[0], here_ref[1]
    core = col % 2
    keep_ref[...] = jnp.zeros(keep_ref.shape, jnp.float32)
    give_ref[...] = jnp.zeros(give_ref.shape, jnp.float32)
    for g in range(GROUPS):
        owner = owner_ref[g]
        for s, got_ref in zip(reversed(range(parts)), refs[:parts]):

            @pl.when((owner % n_col == col) & (owner // n_col == row ^ s))
            def _():
                keep_ref[g] = got_ref[pl.ds(core * half, half), :]
                give_ref[g] = got_ref[pl.ds((1 - core) * half, half), :]


def pick(here, owner, got, tokens, n_col):
    half = got[0].shape[0] // 2
    shape = jax.ShapeDtypeStruct((GROUPS, half, LANES), jnp.float32)
    return pl.pallas_call(
        functools.partial(pick_kernel, n_col, len(got)),
        out_shape=(shape, shape),
        in_specs=[smem(), smem()] + [vmem()] * (len(got) + len(tokens)),
        out_specs=(vmem(), vmem()),
        compiler_params=params(8),
        name="pick",
    )(here, owner, *got, *tokens)


def fetch_vectors(here, owner, stored, slab, width):
    parts, n_col = lax.axis_size("row"), lax.axis_size("col")
    rows = deal(here, stored.reshape(-1, LANES), parts)
    got = [swap(rows[s], "row", s) for s in reversed(range(1, parts))] + [rows[0]]
    half = width // 2
    held, token = load(slab, 0, half, width)
    keep, give = pick(here, owner, got, [token], n_col)
    keep = keep + swap(give, "col", 1)
    held, token = load(slab, half, width - half, width, held, keep)
    bit = 2
    while bit < n_col:
        keep = keep + swap(keep, "col", bit) + token
        bit *= 2
    return keep, swap(keep, "col", 1), held


def first_lanes(parity, group, lane):
    return jnp.where(lane >= offset_of(group), 1, 0) != parity


def spread(pairs, tiles_ref):
    half = pairs.shape[0]
    tiles_ref[pl.ds(0, half, stride=2), :] = pairs
    tiles_ref[pl.ds(1, half, stride=2), :] = pltpu.roll(pairs, BAND, 1)
    return tiles_ref[...]


def lane_grid():
    lane = lax.broadcasted_iota(jnp.int32, (LANES, LANES), 0)
    col = lax.broadcasted_iota(jnp.int32, (LANES, LANES), 1)
    return lane, col


def sum_into(product, hit):
    ones = jnp.where(hit, 1.0, 0.0).astype(jnp.float32)
    return jnp.dot(product, ones, precision=HIGH, preferred_element_type=jnp.float32)


def collect_kernel(here_ref, keep_ref, other_ref, v_ref, sums_ref, norms_ref, tiles_ref):
    half = keep_ref.shape[1]
    core, parity = here_ref[0] % 2, here_ref[1] % 2
    lane, col = lane_grid()
    sums = jnp.zeros(sums_ref.shape, jnp.float32)
    for g in range(GROUPS):
        v_ref[g, pl.ds(core * half, half), :] = keep_ref[g]
        v_ref[g, pl.ds((1 - core) * half, half), :] = other_ref[g]
        tiles = spread(v_ref[g], tiles_ref.at[g])
        spot = jnp.where(first_lanes(parity, g, lane), g, GROUPS + g)
        sums += sum_into(tiles * tiles, (lane < BAND) & (col == spot))
    sums_ref[...] = sums
    turned = jnp.transpose(sums)[:8]
    norms_ref[0] = turned
    norms_ref[1] = pltpu.roll(turned, GROUPS, 0)


def collect(here, keep, other):
    _, half, _ = keep.shape
    tiles = 4 * half
    return pl.pallas_call(
        collect_kernel,
        out_shape=(
            jax.ShapeDtypeStruct((GROUPS, 2 * half, LANES), jnp.float32),
            jax.ShapeDtypeStruct((tiles, LANES), jnp.float32),
            jax.ShapeDtypeStruct((2, 8, tiles), jnp.float32),
        ),
        in_specs=[smem(), vmem(), vmem()],
        out_specs=(vmem(), vmem(), vmem()),
        scratch_shapes=[pltpu.VMEM((GROUPS, tiles, LANES), jnp.float32)],
        compiler_params=params(8),
        name="collect",
    )(here, keep, other)


def table_kernel(here_ref, v_ref, token_ref, table_ref, tiles_ref):
    parity = here_ref[1] % 2
    lane, col = lane_grid()
    first = [first_lanes(parity, g, lane) for g in range(GROUPS)]
    tiles = [spread(v_ref[g], tiles_ref.at[g]) for g in range(GROUPS)]
    table = jnp.zeros(table_ref.shape, jnp.float32)
    for at, (g, h) in enumerate(PAIRS):
        spot = 4 * at + jnp.where(first[g], 0, 2) + jnp.where(first[h], 0, 1)
        table += sum_into(tiles[g] * tiles[h], (lane < BAND) & (col == spot))
    table_ref[...] = table


def make_table(here, v, token):
    tiles = 2 * v.shape[1]
    return pl.pallas_call(
        table_kernel,
        out_shape=jax.ShapeDtypeStruct((tiles, LANES), jnp.float32),
        in_specs=[smem(), vmem(), pl.BlockSpec(memory_space=pl.ANY)],
        out_specs=vmem(),
        scratch_shapes=[pltpu.VMEM((GROUPS, tiles, LANES), jnp.float32)],
        compiler_params=params(8),
        name="table",
    )(here, v, token)


def load_kernel(start, width, x_ref, *refs):
    out_ref, token_ref, sems = refs[-3:]
    rows = width // LOADS
    first = out_ref.shape[0] - width if len(refs) > 3 else 0
    copies = [
        pltpu.make_async_copy(
            x_ref.at[pl.ds(start + i * rows, rows)], out_ref.at[pl.ds(first + i * rows, rows)], sems.at[i]
        )
        for i in range(LOADS)
    ]
    for copy in copies:
        copy.start()
    token_ref[...] = jnp.zeros(token_ref.shape, jnp.float32)
    for copy in copies:
        copy.wait()


def load(slab, start, width, total, into=None, after=None):
    given = [] if into is None else [into, after]
    return pl.pallas_call(
        functools.partial(load_kernel, start, width),
        out_shape=(
            jax.ShapeDtypeStruct((total, slab.shape[1]), slab.dtype),
            jax.ShapeDtypeStruct((8, LANES) if after is None else after.shape, jnp.float32),
        ),
        in_specs=[pl.BlockSpec(memory_space=pltpu.HBM)]
        + [vmem(), pl.BlockSpec(memory_space=pl.ANY)][: len(given)],
        out_specs=(vmem(), vmem()),
        scratch_shapes=[pltpu.SemaphoreType.DMA((LOADS,))],
        input_output_aliases={1: 0} if given else {},
        compiler_params=params(8),
        cost_estimate=pl.CostEstimate(flops=0, bytes_accessed=8 * width * slab.shape[1], transcendentals=0),
        name="load",
    )(slab, *given)


def piece_masks(parity):
    lane = lax.broadcasted_iota(jnp.int32, (8, BLOCK), 1)
    tile = lax.broadcasted_iota(jnp.int32, (8, BLOCK), 0)
    own = lane // BAND == tile
    hits = [first_lanes(parity, g, lane % BAND) for g in range(GROUPS)]
    first = [jnp.where(own & hit, 1.0, 0.0).astype(jnp.float32) for hit in hits]
    second = [jnp.where(own & jnp.logical_not(hit), 1.0, 0.0).astype(jnp.float32) for hit in hits]
    return first, second


def pieces(masks, v_ref, block):
    rows = BLOCK // LANES
    wide = [
        jnp.concatenate(
            [jnp.broadcast_to(v_ref[g, pl.ds(rows * block + j, 1), :], (8, LANES)) for j in range(rows)], axis=1
        )
        for g in range(GROUPS)
    ]
    return jnp.concatenate([m * w for kind in masks for m, w in zip(kind, wide)], axis=0)


def split(x):
    high = x.astype(jnp.bfloat16)
    return high, (x - high.astype(jnp.float32)).astype(jnp.bfloat16)


def products_kernel(lead, start, *refs):
    if lead:
        here_ref, v_ref, held_ref, norms_ref, slab_ref = refs[:5]
        one_ref, two_ref, rest_ref, weights_ref, next_ref, sems = refs[5:]
        masks = piece_masks(here_ref[1] % 2)
        rows = next_ref.shape[0] // LOADS
        copies = [
            pltpu.make_async_copy(
                slab_ref.at[pl.ds(start + i * rows, rows)], next_ref.at[pl.ds(i * rows, rows)], sems.at[i]
            )
            for i in range(LOADS)
        ]
        for copy in copies:
            copy.start()
    else:
        held_ref, weights_ref, one_ref, two_ref, rest_ref = refs
    width, columns = held_ref.shape
    tiles = columns // BAND

    def step(block):
        if lead:
            w_both = jnp.concatenate(split(pieces(masks, v_ref, block)), axis=0)
            weights_ref[block] = w_both
        else:
            w_both = weights_ref[block]
        x_high, x_low = split(held_ref[:, pl.ds(block * BLOCK, BLOCK)])
        across = (((1,), (1,)), ((), ()))
        if width <= LANES:
            both = lax.dot_general(
                w_both, jnp.concatenate([x_high, x_low], axis=0), across, preferred_element_type=jnp.float32
            )
            sums = both[:64, :width] + (both[64:, :width] + both[:64, width:])
        else:
            both = lax.dot_general(w_both, x_high, across, preferred_element_type=jnp.float32)
            low = lax.dot_general(w_both[:64], x_low, across, preferred_element_type=jnp.float32)
            sums = both[:64] + both[64:] + low
        spot = pl.ds(block * 8, 8)
        one_ref[spot, :] = sums[0:8]
        two_ref[spot, :] = sums[32:40]
        for g in range(1, GROUPS):
            rest_ref[g - 1, spot, :] = sums[8 * g : 8 * g + 8]
            rest_ref[g + 2, spot, :] = sums[32 + 8 * g : 40 + 8 * g]

    blocks = columns // BLOCK
    pl.loop(0, blocks, unroll=min(blocks, UNROLL if lead else 2 * UNROLL))(step)
    if lead:
        for at in range(norms_ref.shape[0]):
            one_ref[tiles + 8 * at : tiles + 8 * at + 8] = norms_ref[at, 0]
            two_ref[tiles + 8 * at : tiles + 8 * at + 8] = norms_ref[at, 1]
        for copy in copies:
            copy.wait()


def products(inputs, held, extra=0, start=None, rows=None):
    width, tiles = held.shape[0], held.shape[1] // BAND
    lead = start is not None
    message = jax.ShapeDtypeStruct((tiles + extra, width), jnp.float32)
    shapes = [message, message, jax.ShapeDtypeStruct((2 * GROUPS - 2, tiles, width), jnp.float32)]
    specs = [vmem()] * len(inputs)
    if lead:
        shapes.append(jax.ShapeDtypeStruct((tiles // 8, 128, BLOCK), jnp.bfloat16))
        shapes.append(jax.ShapeDtypeStruct((rows, held.shape[1]), jnp.float32))
        specs = [smem(), vmem(), vmem(), vmem(), pl.BlockSpec(memory_space=pltpu.HBM)]
    return pl.pallas_call(
        functools.partial(products_kernel, lead, start),
        out_shape=tuple(shapes),
        in_specs=specs,
        out_specs=(vmem(),) * len(shapes),
        scratch_shapes=[pltpu.SemaphoreType.DMA((LOADS,))] if lead else [],
        compiler_params=params(8),
        cost_estimate=pl.CostEstimate(
            flops=2 * 192 * width * held.shape[1], bytes_accessed=4 * width * held.shape[1], transcendentals=0
        ),
        name="products",
    )(*inputs)


def align(x, here_ref):
    back = jnp.concatenate([x[1:], x[:1]], axis=0)
    on = jnp.concatenate([x[-1:], x[:-1]], axis=0)
    return jnp.where(here_ref[1] == 0, on, jnp.where(here_ref[1] == here_ref[2] - 1, back, x))


def scales_of(here_ref, sums_ref, got_one_ref, got_two_ref):
    tiles = sums_ref.shape[0]
    got = []
    for ref in (got_one_ref, got_two_ref):
        rows = [ref[at : at + 8, :] for at in range(tiles, ref.shape[0], 8)]
        rows = jnp.concatenate(rows, axis=1)[:, :tiles]
        got.append(jnp.transpose(jnp.concatenate([rows] + [jnp.zeros_like(rows)] * (LANES // 8 - 1), axis=0)))
    row = lax.broadcasted_iota(jnp.int32, (tiles, LANES), 0)
    gone = ((here_ref[1] == 0) & (row == 0)) | ((here_ref[1] == here_ref[2] - 1) & (row == tiles - 1))
    col = lax.broadcasted_iota(jnp.int32, (tiles, LANES), 1)
    other = jnp.where(col < GROUPS, got[0], pltpu.roll(align(got[1], here_ref), GROUPS, 1))
    tau = 2.0 / (sums_ref[...] + other + 1e-6)
    return jnp.where(gone & (col >= GROUPS), 0.0, tau)


def solve_kernel(group, lead, here_ref, table_ref, tau_ref, after_ref, *refs):
    refs = list(refs)
    own_one_ref, own_two_ref, got_one_ref, got_two_ref = [refs.pop(0) for _ in range(4)]
    last = group == GROUPS - 1
    tiles = table_ref.shape[0]
    tau = scales_of(here_ref, tau_ref, got_one_ref, got_two_ref) if lead else tau_ref[...]
    one = tau[:, group : group + 1] * (own_one_ref[:tiles] + got_one_ref[:tiles])
    two = tau[:, GROUPS + group : GROUPS + group + 1] * (
        own_two_ref[:tiles] + align(got_two_ref[:tiles], here_ref)
    )
    if last:
        coef_one_ref, coef_two_ref = refs
        coef_one_ref[...] = one
        coef_two_ref[...] = two
        return
    rest_ref = refs.pop(0)
    before = [refs.pop(0) for _ in range(2 * group)]
    coef_one_ref, coef_two_ref = refs.pop(0), refs.pop(0)
    coef_one_ref[...] = one
    coef_two_ref[...] = two
    if lead:
        refs.pop()[...] = tau
    table = table_ref[...]
    later = group + 1
    next_one = rest_ref[later - 1]
    next_two = rest_ref[later + 2]
    for h in range(later):
        at = 4 * PAIRS.index((later, h))
        c_one, c_two = (one, two) if h == group else (before[2 * h][...], before[2 * h + 1][...])
        next_one = next_one - table[:, at : at + 1] * c_one - table[:, at + 1 : at + 2] * c_two
        next_two = next_two - table[:, at + 2 : at + 3] * c_one - table[:, at + 3 : at + 4] * c_two
    refs[0][...] = next_one
    refs[1][...] = next_two


def solve(here, table, tau, own, got, rest, before, group, after, lead=False):
    tiles, width = table.shape[0], got[0].shape[1]
    last = group == GROUPS - 1
    inputs = [here, table, tau, after] + list(own) + list(got)
    shapes = [jax.ShapeDtypeStruct((tiles, width), jnp.float32)] * 2
    if not last:
        inputs += [rest] + [c for pair in before for c in pair]
        shapes += [jax.ShapeDtypeStruct((tiles, width), jnp.float32)] * 2
    if lead:
        shapes.append(jax.ShapeDtypeStruct((tiles, LANES), jnp.float32))
    return pl.pallas_call(
        functools.partial(solve_kernel, group, lead),
        out_shape=tuple(shapes),
        in_specs=[smem(), vmem(), vmem(), pl.BlockSpec(memory_space=pl.ANY)] + [vmem()] * (len(inputs) - 4),
        out_specs=tuple(vmem() for _ in shapes),
        compiler_params=params(8),
        cost_estimate=pl.CostEstimate(flops=tiles, bytes_accessed=4 * tiles, transcendentals=0),
        name="solve",
    )(*inputs)


def update_kernel(start, weights_ref, x_ref, *refs):
    out_ref, token_ref, stage_ref, sems = refs[-4:]
    slots, width, span = stage_ref.shape
    token_ref[...] = jnp.zeros(token_ref.shape, jnp.float32)

    def write(slot, step):
        to = out_ref.at[pl.ds(start, width), pl.ds(step * span, span)]
        return pltpu.make_async_copy(stage_ref.at[slot], to, sems.at[slot])

    for step in range(x_ref.shape[1] // span):
        slot = step % slots
        if step >= slots:
            write(slot, step - slots).wait()
        for part in range(span // BLOCK):
            block = step * (span // BLOCK) + part
            spot = pl.ds(block * 8, 8)
            c_high, c_low = split(jnp.concatenate([ref[spot, :] for ref in refs[: 2 * GROUPS]], axis=0))
            w_both = weights_ref[block]
            change = lax.dot_general(
                jnp.concatenate([c_high, c_high, c_low], axis=0),
                jnp.concatenate([w_both, w_both[:64]], axis=0),
                (((0,), (0,)), ((), ())),
                preferred_element_type=jnp.float32,
            )
            here = slice(block * BLOCK, (block + 1) * BLOCK)
            stage_ref[slot, :, part * BLOCK : (part + 1) * BLOCK] = x_ref[:, here] - change
        write(slot, step).start()
    steps = x_ref.shape[1] // span
    for step in range(max(0, steps - slots), steps):
        write(step % slots, step).wait()


def update(weights, held, coefs, result, start, total):
    width = held.shape[0]
    span = min(STEP // width, held.shape[1])
    inputs = [weights, held] + [c[0] for c in coefs] + [c[1] for c in coefs]
    specs = [vmem()] * len(inputs)
    alias = {}
    if result is not None:
        alias = {len(inputs): 0}
        inputs.append(result)
        specs.append(pl.BlockSpec(memory_space=pl.ANY))
    return pl.pallas_call(
        functools.partial(update_kernel, start),
        out_shape=(
            jax.ShapeDtypeStruct((total, held.shape[1]), jnp.float32),
            jax.ShapeDtypeStruct((8, LANES), jnp.float32),
        ),
        in_specs=specs,
        out_specs=(pl.BlockSpec(memory_space=pltpu.HBM), vmem()),
        scratch_shapes=[pltpu.VMEM((SLOTS, width, span), jnp.float32), pltpu.SemaphoreType.DMA((SLOTS,))],
        input_output_aliases=alias,
        compiler_params=params(8),
        cost_estimate=pl.CostEstimate(
            flops=2 * 192 * width * held.shape[1], bytes_accessed=8 * width * held.shape[1], transcendentals=0
        ),
        name="update",
    )(*inputs)


def shards(slab, stored, owner):
    parts = lax.axis_size("row")
    total, rows = slab.shape
    tiles = rows // BAND
    width = total // 2
    here = [lax.axis_index("col"), lax.axis_index("row"), jnp.int32(parts)]
    here = jnp.stack(here).astype(jnp.int32)
    keep, other, held = fetch_vectors(here, owner, stored, slab, width)
    v, sums, norms = collect(here, keep, other)
    if tiles < width:
        norms = jnp.pad(norms, ((0, 0), (0, 0), (0, width - tiles)))
    norms = norms.reshape(2, 8, -1, width).transpose(2, 0, 1, 3)
    first = products([here, v, held, norms, slab], held, 8 * norms.shape[0], width, total - width)
    weights = first[3]
    held = [held, first[4]]
    second = products([held[1], weights], held[1])
    table = make_table(here, v, second[2])
    own, rest, coefs = [first[:2], second[:2]], [first[2], second[2]], [[], []]
    tau, after = sums, table
    for group in range(GROUPS - 1):
        for i in range(2):
            got = (swap_first(own[i][0]), swap_second(own[i][1]))
            lead = group == 0 and i == 0
            outs = solve(here, table, tau, own[i], got, rest[i], coefs[i], group, after, lead)
            coefs[i].append(outs[:2])
            own[i] = outs[2:4]
            after = outs[0]
            if lead:
                tau = outs[-1]
    result = None
    group = GROUPS - 1
    for i in range(2):
        got = (swap_first(own[i][0]), swap_second(own[i][1]))
        last = solve(here, table, tau, own[i], got, None, None, group, after)
        result, after = update(weights, held[i], coefs[i] + [last], result, i * width, total)
    return result


def solution(mesh):
    placed = (P("col", "row"), P(("row", "col"), None), P())
    return jax.shard_map(
        shards, mesh=mesh, in_specs=placed, out_specs=P("col", "row"), check_vma=False
    )
```
